256 devices in a mesh: resp: 16 (over y, z_hi), ctx: 16 (over x, z_lo, core).
Axes of the slice: x: 4, y: 4, z: 8 (z_hi: 4, z_lo: 2; z = z_hi * 2 + z_lo), core: 2. Of those that a mesh axis runs over, the one named last changes fastest.
Arguments:
- queries: bfloat16 [16, 2048, 2560], P('resp', 'ctx'), may hold values from -96 to 96
- resp_keys: bfloat16 [16, 2048, 512], P('resp', 'ctx'), may hold values from -6 to 6
- resp_values: bfloat16 [16, 2048, 512], P('resp', 'ctx'), may hold values from -6 to 6
- prompt_keys: bfloat16 [512, 512], P('ctx'), may hold values from -6 to 6
- prompt_values: bfloat16 [512, 512], P('ctx'), may hold values from -6 to 6
- out_grad: bfloat16 [16, 2048, 2560], P('resp', 'ctx'), may hold values from -24 to 24
- lengths: int32 [16], P('resp'), may hold values from 256 to 2048, as said below
Outputs:
- attn_out: bfloat16 [16, 2048, 2560], P('resp', 'ctx')
- query_grad: bfloat16 [16, 2048, 2560], P('resp', 'ctx')
- resp_key_grad: bfloat16 [16, 2048, 512], P('resp', 'ctx')
- resp_value_grad: bfloat16 [16, 2048, 512], P('resp', 'ctx')
- prompt_key_grad: bfloat16 [512, 512], P('ctx')
- prompt_value_grad: bfloat16 [512, 512], P('ctx')
The draws below stay inside these ranges and needn't reach their ends.
Inputs may be any that keep to these rules, and one draw needn't show every extreme that they name: `lengths`: some response has all 2048 tokens.
All inputs are finite; a program needn't handle non-finite values.
Results may differ from the reference program's by a relative error of at most 0.023.
Values may be sent and summed in bfloat16 or wider, within the bound.
A program may use at most 128 MiB of HBM per device.

```python
import jax
import jax.numpy as jnp
from jax import lax

DH = 128
HQ = 20
HK = 4
RESP = 16
SEQ = 2048
PROMPT = 512


def draw_prompt_keys(key, part):
    entries = jax.random.normal(jax.random.fold_in(key, 5), (PROMPT, HK * DH), jnp.float32)
    return jnp.clip(entries, -6.0, 6.0).astype(jnp.bfloat16)


def draw_queries(key, part):
    entries = jax.random.normal(jax.random.fold_in(key, 3), (RESP, SEQ, HQ * DH), jnp.float32)
    entries = jnp.clip(entries, -6.0, 6.0)
    return entries.astype(jnp.bfloat16)


def draw_lengths(key, part):
    drawn = jax.random.randint(jax.random.fold_in(key, 11), (RESP,), SEQ // 8, SEQ + 1)
    longest = jax.random.randint(jax.random.fold_in(key, 13), (), 0, RESP)
    return jnp.where(jnp.arange(RESP) == longest, SEQ, drawn).astype(jnp.int32)


def block_levels(rng, dims, shards, low, high):
    factor_of = 1.0
    for dim, shards_of in shards:
        draws = jax.random.uniform(jax.random.fold_in(jax.random.fold_in(rng, 6), dim), (shards_of,), jnp.float32, low / len(shards), high / len(shards))
        factor_of = factor_of * jnp.repeat(jnp.exp(draws), dims[dim] // shards_of).reshape((-1,) + (1,) * (len(dims) - 1 - dim))
    return factor_of


def noise(key, shape, deviation, reach, cuts=(), kind=jnp.bfloat16):
    values = deviation * jax.random.normal(key, shape, jnp.float32)
    if cuts:
        values = values * block_levels(key, shape, cuts, -0.22, 0.18)
    return jnp.clip(values, -reach, reach).astype(kind)


def setup_inputs(seed: int = 0) -> dict:
    key_list = jax.random.split(jax.random.key(seed), 8)
    return {
        "queries": draw_queries(jax.random.fold_in(key_list[7], 71), 0),
        "resp_keys": noise(key_list[1], (RESP, SEQ, HK * DH), 1.0, 6.0, ((0, 16), (1, 16))),
        "resp_values": noise(key_list[2], (RESP, SEQ, HK * DH), 1.0, 6.0, ((0, 16), (1, 16))),
        "prompt_keys": draw_prompt_keys(jax.random.fold_in(key_list[7], 71), 0),
        "prompt_values": noise(key_list[4], (PROMPT, HK * DH), 1.0, 6.0, ((0, 16),)),
        "out_grad": noise(key_list[5], (RESP, SEQ, HQ * DH), 4.0, 24.0, ((0, 16), (1, 16))),
        "lengths": draw_lengths(jax.random.fold_in(key_list[7], 71), 0),
    }


NEG = -1.0e30


def attend(query_block, grad_block, row_pos, row_ok, keys_all, values_all, key_pos):
    count = query_block.shape[0]
    total = keys_all.shape[0]
    group = HQ // HK
    scale = DH ** -0.5
    query32 = query_block.astype(jnp.float32).reshape(count, HK, group, DH)
    keys32 = keys_all.astype(jnp.float32).reshape(total, HK, DH)
    values32 = values_all.astype(jnp.float32).reshape(total, HK, DH)
    raw = jnp.einsum('nkgd,mkd->kgnm', query32, keys32) * scale
    allowed = key_pos[None, :] <= row_pos[:, None]
    scores = jnp.where(allowed[None, None], raw, jnp.float32(NEG))
    top = jnp.max(scores, axis=-1)
    lse = top + jnp.log(jnp.sum(jnp.exp(scores - top[..., None]), axis=-1))
    prob = jnp.exp(scores - lse[..., None])
    prob_low = lax.optimization_barrier(prob.astype(jnp.bfloat16)).astype(jnp.float32)
    mixed = jnp.einsum('kgnm,mkd->nkgd', prob_low, values32).reshape(count, HQ * DH)
    out = jnp.where(row_ok[:, None], mixed, jnp.float32(0.0)).astype(jnp.bfloat16)
    grad = jnp.where(row_ok[:, None], grad_block, jnp.zeros_like(grad_block))
    grad32 = grad.astype(jnp.float32).reshape(count, HK, group, DH)
    out32 = out.astype(jnp.float32).reshape(count, HK, group, DH)
    delta = jnp.einsum('nkgd,nkgd->kgn', grad32, out32)
    dprob = jnp.einsum('nkgd,mkd->kgnm', grad32, values32)
    dscore = lax.optimization_barrier((prob * (dprob - delta[..., None])).astype(jnp.bfloat16)).astype(jnp.float32)
    dquery = (jnp.einsum('kgnm,mkd->nkgd', dscore, keys32) * scale).reshape(count, HQ * DH)
    dkey = (jnp.einsum('kgnm,nkgd->mkd', dscore, query32) * scale).reshape(total, HK * DH)
    dvalue = jnp.einsum('kgnm,nkgd->mkd', prob_low, grad32).reshape(total, HK * DH)
    return out, dquery.astype(jnp.bfloat16), dkey, dvalue


def reference(queries, resp_keys, resp_values, prompt_keys, prompt_values, out_grad, lengths):
    block = min(SEQ, 512)
    blocks = SEQ // block
    key_pos = jnp.concatenate([jnp.full((PROMPT,), -1, jnp.int32), jnp.arange(SEQ).astype(jnp.int32)])

    def one(items):
        query_r, key_r, value_r, grad_r, length_r = items
        keys_all = jnp.concatenate([prompt_keys, key_r], axis=0)
        values_all = jnp.concatenate([prompt_values, value_r], axis=0)

        def step(acc, index):
            start = (index * block).astype(jnp.int32)
            query_block = lax.dynamic_slice_in_dim(query_r, start, block, 0)
            grad_block = lax.dynamic_slice_in_dim(grad_r, start, block, 0)
            row_pos = start + jnp.arange(block).astype(jnp.int32)
            row_ok = row_pos < length_r
            out, dquery, dkey, dvalue = attend(query_block, grad_block, row_pos, row_ok, keys_all, values_all, key_pos)
            return (acc[0] + dkey, acc[1] + dvalue), (out, dquery)

        zero = jnp.zeros((PROMPT + SEQ, HK * DH), jnp.float32)
        (dkey, dvalue), (outs, dqueries) = lax.scan(step, (zero, zero), jnp.arange(blocks).astype(jnp.int32))
        return outs.reshape(SEQ, HQ * DH), dqueries.reshape(SEQ, HQ * DH), dkey, dvalue

    outs, dqueries, dkeys, dvalues = lax.map(one, (queries, resp_keys, resp_values, out_grad, lengths))
    resp_key_grad = dkeys[:, PROMPT:].astype(jnp.bfloat16)
    resp_value_grad = dvalues[:, PROMPT:].astype(jnp.bfloat16)
    prompt_key_grad = jnp.sum(dkeys[:, :PROMPT], axis=0).astype(jnp.bfloat16)
    prompt_value_grad = jnp.sum(dvalues[:, :PROMPT], axis=0).astype(jnp.bfloat16)
    return (outs, dqueries, resp_key_grad, resp_value_grad, prompt_key_grad, prompt_value_grad)
```

```python
import functools
import math

import jax
import jax.numpy as jnp
from jax import lax
from jax.experimental import pallas as pl
from jax.experimental.pallas import tpu as pltpu
from jax.sharding import PartitionSpec as P

DH = 128
HQ = 20
HK = 4
G = HQ // HK
GW = G * DH
R = 128
M = G * R
CH = 512
NC = 5
PR = 32
BF = jnp.bfloat16
F32 = jnp.float32
MESH = pl.DeviceIdType.MESH
SCALE = DH**-0.5
CEXP = SCALE * math.log2(math.e)
NEG = -1e30
NT = (((1,), (1,)), ((), ()))
NN = (((1,), (0,)), ((), ()))


def dot(a, b, dims):
    return lax.dot_general(a, b, dims, preferred_element_type=F32)


def rows_of(i, size):
    return pl.ds(pl.multiple_of(i * size, size), size)


def attend_block(b, j, length, qin, gin, kbuf, ob, dqb, qs, gs, s_scr, p_scr, dkt, dvt):
    for h in range(G):
        qs[h * R : (h + 1) * R, :] = qin[b, :, h * DH : (h + 1) * DH]
    q = qs[...]

    def scores(k, m):
        s = dot(q, kbuf[0, k], NT)
        s_scr[k] = s
        for t in range(CH // 128):
            m = jnp.maximum(m, s[:, t * 128 : (t + 1) * 128])
        return m

    m = lax.fori_loop(0, b + 1, scores, jnp.full((M, 128), NEG, F32))
    last = b + 1
    s = dot(q, kbuf[0, last], NT)
    row = lax.broadcasted_iota(jnp.int32, (R, CH), 0) + j * R
    col = lax.broadcasted_iota(jnp.int32, (R, CH), 1)
    s = jnp.where(jnp.concatenate([col <= row] * G, axis=0), s, NEG)
    s_scr[last] = s
    for t in range(CH // 128):
        m = jnp.maximum(m, s[:, t * 128 : (t + 1) * 128])
    top = jnp.max(m, axis=1, keepdims=True) * CEXP

    def mix(k, carry):
        o, l = carry
        p = jnp.exp2(s_scr[k] * CEXP - top)
        for t in range(CH // 128):
            l = l + p[:, t * 128 : (t + 1) * 128]
        p = p.astype(BF)
        p_scr[k] = p
        return o + dot(p, kbuf[1, k], NN), l

    o, l = lax.fori_loop(0, b + 2, mix, (jnp.zeros((M, DH), F32), jnp.zeros((M, 128), F32)))
    rl = 1.0 / jnp.sum(l, axis=1, keepdims=True)
    token = lax.broadcasted_iota(jnp.int32, (R, 1), 0) + (4 * b + j) * R
    valid = jnp.concatenate([token < length] * G, axis=0)
    o = jnp.where(valid, o * rl, 0.0).astype(BF)
    for h in range(G):
        ob[b, :, h * DH : (h + 1) * DH] = o[h * R : (h + 1) * R, :]
        gs[h * R : (h + 1) * R, :] = gin[b, :, h * DH : (h + 1) * DH]
    gl = jnp.where(valid, gs[...].astype(F32) * rl, 0.0).astype(BF)
    delta = jnp.sum(gl.astype(F32) * o.astype(F32), axis=1, keepdims=True)
    qt = q.astype(F32).T.astype(BF)
    gt = gl.astype(F32).T.astype(BF)

    def grads(k, dq):
        kc = kbuf[0, k]
        p = p_scr[k]
        dp = dot(gl, kbuf[1, k], NT)
        ds = (p.astype(F32) * (dp - delta)).astype(BF)
        dvt[k] += dot(gt, p, NN)
        dkt[k] += dot(qt, ds, NN)
        return dq + dot(ds, kc, NN)

    dq = lax.fori_loop(0, b + 2, grads, jnp.zeros((M, DH), F32))
    dq = (dq * SCALE).astype(BF)
    for h in range(G):
        dqb[b, :, h * DH : (h + 1) * DH] = dq[h * R : (h + 1) * R, :]


def kernel(
    n,
    len_ref, q_ref, rk_ref, rv_ref, pk_ref, pv_ref, g_ref,
    out_ref, dq_ref, drk_ref, drv_ref, dpk_ref, dpv_ref,
    qin, gin, kbuf, ob, dqb, qs, gs, s_scr, p_scr, dkt, dvt,
    s1, r1, s2, r2, s3, ps, pin, pown, pall,
    loc, kv_send, kv_recv, qg_send, qg_recv, f_send, f_recv, o_send, o_recv,
    c_send, c_recv, x_send, x_recv, rs_send, rs_recv, ag_send, ag_recv, px_send, px_recv,
    fin,
):
    c = lax.axis_index("ctx")
    r = lax.axis_index("resp")
    x, j = c // 4, c % 4
    zl, core = j // 2, j % 2
    core_mate = x * 4 + zl * 2 + (1 - core)
    z_mate = x * 4 + (1 - zl) * 2 + core
    j_c = zl * 2 + (1 - core)
    j_z = (1 - zl) * 2 + core
    ORDER = (1, 3, 2)
    prow = 256 // n

    def other(d):
        return (x + d) % 4

    def source(d):
        return (x + 4 - d) % 4

    def send(src, dst, ssem, rsem, **where):
        return pltpu.make_async_remote_copy(
            src_ref=src, dst_ref=dst, send_sem=ssem, recv_sem=rsem,
            device_id=where, device_id_type=MESH,
        )

    barrier = pltpu.get_barrier_semaphore()
    for d in ORDER:
        pl.semaphore_signal(barrier, inc=1, device_id={"ctx": other(d) * 4 + j}, device_id_type=MESH)
    for mate in (core_mate, z_mate):
        pl.semaphore_signal(barrier, inc=1, device_id={"ctx": mate}, device_id_type=MESH)
    for e in range(1, n):
        pl.semaphore_signal(barrier, inc=1, device_id={"resp": (r + e) % n}, device_id_type=MESH)
    pl.semaphore_wait(barrier, 5 + n - 1)

    def head_cols(h):
        return rows_of(h, DH)

    def kv_pairs(h, at):
        cols = head_cols(h)
        rows = rows_of(j, R)
        prows = pl.ds(pl.multiple_of(j * R + at * PR, PR), PR)
        return (
            (rk_ref.at[0, :, cols], kbuf.at[0, 1 + at, rows, :]),
            (rv_ref.at[0, :, cols], kbuf.at[1, 1 + at, rows, :]),
            (pk_ref.at[:, cols], kbuf.at[0, 0, prows, :]),
            (pv_ref.at[:, cols], kbuf.at[1, 0, prows, :]),
        )

    kv_copies = {}
    for d in ORDER:
        kv_copies[d] = [
            send(src, dst, kv_send.at[d - 1, i], kv_recv.at[d - 1, i], ctx=other(d) * 4 + j)
            for i, (src, dst) in enumerate(kv_pairs(other(d), x))
        ]
        for cp in kv_copies[d]:
            cp.start()
    own = [pltpu.make_async_copy(src, dst, loc.at[i]) for i, (src, dst) in enumerate(kv_pairs(x, x))]
    for cp in own:
        cp.start()

    def qg_pairs(h, at):
        cols = rows_of(h, GW)
        return ((q_ref.at[0, :, cols], qin.at[at]), (g_ref.at[0, :, cols], gin.at[at]))

    qg_copies = []
    for d in ORDER:
        for i, (src, dst) in enumerate(qg_pairs(other(d), x)):
            cp = send(src, dst, qg_send.at[d, i], qg_recv.at[d, i], ctx=other(d) * 4 + j)
            cp.start()
            qg_copies.append(cp)
    for i, (src, dst) in enumerate(qg_pairs(x, x)):
        pltpu.make_async_copy(src, dst, qg_recv.at[0, i]).start()

    fwd = []

    def hand_on(slot, chunk, rows_j, kind, mate):
        view = kbuf.at[:, chunk, rows_of(rows_j, R), :]
        cp = send(view, view, f_send.at[slot, kind], f_recv.at[slot, kind], ctx=mate)
        cp.start()
        fwd.append(cp)

    def wait_handed(slot, chunk, rows_j, kind, mate):
        view = kbuf.at[:, chunk, rows_of(rows_j, R), :]
        send(view, view, f_send.at[slot, kind], f_recv.at[slot, kind], ctx=mate).wait_recv()

    for cp in own:
        cp.wait()
    hand_on(0, 1 + x, j, 0, core_mate)
    hand_on(0, 1 + x, j, 1, z_mate)
    for d in ORDER:
        for i, (src, dst) in enumerate(kv_pairs(x, source(d))):
            send(src, dst, kv_send.at[d - 1, i], kv_recv.at[d - 1, i], ctx=c).wait_recv()
        hand_on(d, 1 + source(d), j, 0, core_mate)
        hand_on(d, 1 + source(d), j, 1, z_mate)
    hand_on(4, 0, j, 0, core_mate)
    hand_on(4, 0, j, 1, z_mate)
    slots = [(0, 1 + x)] + [(d, 1 + source(d)) for d in ORDER] + [(4, 0)]
    for slot, chunk in slots:
        wait_handed(slot, chunk, j_z, 1, z_mate)
        hand_on(slot, chunk, j_z, 2, core_mate)
    for slot, chunk in slots:
        wait_handed(slot, chunk, j_c, 0, core_mate)
        wait_handed(slot, chunk, 3 - j, 2, core_mate)

    dkt[...] = jnp.zeros_like(dkt)
    dvt[...] = jnp.zeros_like(dvt)
    length = len_ref[0]

    def result_pairs(b, h):
        cols = rows_of(h, GW)
        return ((ob.at[b], out_ref.at[0, :, cols]), (dqb.at[b], dq_ref.at[0, :, cols]))

    def step(i, carry):
        d = jnp.where(i == 0, 1, jnp.where(i == 1, 3, jnp.where(i == 2, 2, 0)))
        b = (x + 4 - d) % 4
        for t, (src, dst) in enumerate(qg_pairs(x, b)):
            pltpu.make_async_copy(src, dst, qg_recv.at[d, t]).wait()
        attend_block(b, j, length, qin, gin, kbuf, ob, dqb, qs, gs, s_scr, p_scr, dkt, dvt)

        @pl.when(i < 3)
        def _():
            for t, (src, dst) in enumerate(result_pairs(b, x)):
                send(src, dst, o_send.at[d, t], o_recv.at[d, t], ctx=b * 4 + j).start()

        return carry

    lax.fori_loop(0, 4, step, 0)
    finals = []
    for t, (src, dst) in enumerate(result_pairs(x, x)):
        cp = pltpu.make_async_copy(src, dst, fin.at[t])
        cp.start()
        finals.append(cp)

    def part(k, kv, jj):
        lanes = rows_of(jj, R)
        if kv == 0:
            return dkt[k, :, lanes].T * SCALE
        return dvt[k, :, lanes].T

    for k in range(NC):
        for kv in range(2):
            for zz in range(2):
                s1[zz, kv, k] = part(k, kv, 2 * zz + 1 - core).astype(BF)
    cp1 = send(s1, r1, c_send.at[0], c_recv.at[0], ctx=core_mate)
    cp1.start()
    cp1.wait_recv()
    for k in range(NC):
        for kv in range(2):
            s2[kv, k] = (part(k, kv, j_z) + r1[1 - zl, kv, k].astype(F32)).astype(BF)
    cp2 = send(s2, r2, c_send.at[1], c_recv.at[1], ctx=z_mate)
    cp2.start()
    cp2.wait_recv()

    def total(k, kv):
        return part(k, kv, j) + r1[zl, kv, k].astype(F32) + r2[kv, k].astype(F32)

    for kv in range(2):
        t = total(0, kv)
        pown[kv * R : (kv + 1) * R, :] = t
        ps[kv * R : (kv + 1) * R, :] = t.astype(BF)

    def scatter(e, carry):
        to = (r + e) % n
        send(ps.at[rows_of(to, prow), :], pin.at[e], rs_send.at[e], rs_recv.at[e], resp=to).start()
        return carry

    lax.fori_loop(1, n, scatter, 0)

    for k in range(1, NC):
        for kv in range(2):
            s3[k - 1, kv] = total(k, kv).astype(BF)

    def row_pairs(at, h):
        cols = head_cols(h)
        return ((s3.at[at, 0], drk_ref.at[0, :, cols]), (s3.at[at, 1], drv_ref.at[0, :, cols]))

    xs_copies = []
    for d in ORDER:
        for t, (src, dst) in enumerate(row_pairs(other(d), x)):
            cp = send(src, dst, x_send.at[d, t], x_recv.at[d, t], ctx=other(d) * 4 + j)
            cp.start()
            xs_copies.append(cp)
    for t, (src, dst) in enumerate(row_pairs(x, x)):
        cp = pltpu.make_async_copy(src, dst, fin.at[2 + t])
        cp.start()
        finals.append(cp)

    def gather_sum(e, acc):
        send(ps.at[rows_of(r, prow), :], pin.at[e], rs_send.at[e], rs_recv.at[e], resp=r).wait_recv()
        return acc + pin[e].astype(F32)

    psum = lax.fori_loop(1, n, gather_sum, pown[rows_of(r, prow), :])
    pall[rows_of(r, prow), :] = psum.astype(BF)

    def spread(e, carry):
        to = (r + e) % n
        view = pall.at[rows_of(r, prow), :]
        send(view, view, ag_send.at[e], ag_recv.at[e], resp=to).start()
        return carry

    lax.fori_loop(1, n, spread, 0)

    def collect(e, carry):
        view = pall.at[rows_of((r + n - e) % n, prow), :]
        send(view, view, ag_send.at[e], ag_recv.at[e], resp=r).wait_recv()
        return carry

    lax.fori_loop(1, n, collect, 0)

    def prompt_pairs(at, h):
        cols = head_cols(h)
        return (
            (pall.at[rows_of(at, PR), :], dpk_ref.at[:, cols]),
            (pall.at[rows_of(4 + at, PR), :], dpv_ref.at[:, cols]),
        )

    for d in ORDER:
        for t, (src, dst) in enumerate(prompt_pairs(other(d), x)):
            cp = send(src, dst, px_send.at[d, t], px_recv.at[d, t], ctx=other(d) * 4 + j)
            cp.start()
            xs_copies.append(cp)
    for t, (src, dst) in enumerate(prompt_pairs(x, x)):
        cp = pltpu.make_async_copy(src, dst, fin.at[4 + t])
        cp.start()
        finals.append(cp)

    for d in ORDER:
        for t in range(2):
            src, dst = result_pairs(source(d), other(d))[t]
            cp = send(src, dst, o_send.at[d, t], o_recv.at[d, t], ctx=source(d) * 4 + j)
            cp.wait_recv()
            cp.wait_send()
            src, dst = row_pairs(x, source(d))[t]
            send(src, dst, x_send.at[d, t], x_recv.at[d, t], ctx=c).wait_recv()
            src, dst = prompt_pairs(x, source(d))[t]
            send(src, dst, px_send.at[d, t], px_recv.at[d, t], ctx=c).wait_recv()
    for cp in finals:
        cp.wait()
    for d in ORDER:
        for cp in kv_copies[d]:
            cp.wait_send()
    for cp in qg_copies + fwd + [cp1, cp2] + xs_copies:
        cp.wait_send()

    def sent(e, carry):
        send(ps.at[rows_of(r, prow), :], pin.at[e], rs_send.at[e], rs_recv.at[e], resp=r).wait_send()
        view = pall.at[rows_of(r, prow), :]
        send(view, view, ag_send.at[e], ag_recv.at[e], resp=r).wait_send()
        return carry

    lax.fori_loop(1, n, sent, 0)


def body(n, queries, resp_keys, resp_values, prompt_keys, prompt_values, out_grad, lengths):
    shape = jax.ShapeDtypeStruct
    anywhere = pl.BlockSpec(memory_space=pl.ANY)
    vmem = pltpu.VMEM
    dma = pltpu.SemaphoreType.DMA
    return pl.pallas_call(
        functools.partial(kernel, n),
        out_shape=(
            shape((1, R, HQ * DH), BF),
            shape((1, R, HQ * DH), BF),
            shape((1, R, HK * DH), BF),
            shape((1, R, HK * DH), BF),
            shape((PR, HK * DH), BF),
            shape((PR, HK * DH), BF),
        ),
        in_specs=[pl.BlockSpec(memory_space=pltpu.SMEM)] + [anywhere] * 6,
        out_specs=(anywhere,) * 6,
        scratch_shapes=[
            vmem((4, R, GW), BF), vmem((4, R, GW), BF), vmem((2, NC, CH, DH), BF),
            vmem((4, R, GW), BF), vmem((4, R, GW), BF), vmem((M, DH), BF), vmem((M, DH), BF),
            vmem((NC, M, CH), F32), vmem((NC, M, CH), BF), vmem((NC, DH, CH), F32), vmem((NC, DH, CH), F32),
            vmem((2, 2, NC, R, DH), BF), vmem((2, 2, NC, R, DH), BF),
            vmem((2, NC, R, DH), BF), vmem((2, NC, R, DH), BF), vmem((4, 2, R, DH), BF),
            vmem((2 * R, DH), BF), vmem((n, 256 // n, DH), BF), vmem((2 * R, DH), F32), vmem((2 * R, DH), BF),
            dma((4,)), dma((3, 4)), dma((3, 4)), dma((4, 2)), dma((4, 2)), dma((5, 3)), dma((5, 3)),
            dma((4, 2)), dma((4, 2)), dma((2,)), dma((2,)), dma((4, 2)), dma((4, 2)),
            dma((n,)), dma((n,)), dma((n,)), dma((n,)), dma((4, 2)), dma((4, 2)), dma((6,)),
        ],
        compiler_params=pltpu.CompilerParams(
            collective_id=0, has_side_effects=True, vmem_limit_bytes=56 << 20
        ),
    )(lengths, queries, resp_keys, resp_values, prompt_keys, prompt_values, out_grad)


def solution(mesh):
    seq = P("resp", "ctx", None)
    return jax.shard_map(
        functools.partial(body, mesh.shape["resp"]),
        mesh=mesh,
        in_specs=(seq, seq, seq, P("ctx", None), P("ctx", None), seq, P("resp")),
        out_specs=(seq, seq, seq, seq, P("ctx", None), P("ctx", None)),
        check_vma=False,
    )
```

```python
import functools
import math

import jax
import jax.numpy as jnp
from jax import lax
from jax.experimental import pallas as pl
from jax.experimental.pallas import tpu as pltpu
from jax.sharding import PartitionSpec as P

DH = 128
HQ = 20
HK = 4
G = HQ // HK
GW = G * DH
R = 128
M = G * R
CH = 512
NC = 5
PR = 32
BF = jnp.bfloat16
F32 = jnp.float32
MESH = pl.DeviceIdType.MESH
SCALE = DH**-0.5
CEXP = SCALE * math.log2(math.e)
NEG = -1e30
NT = (((1,), (1,)), ((), ()))
NN = (((1,), (0,)), ((), ()))
TN = (((0,), (0,)), ((), ()))


def dot(a, b, dims):
    return lax.dot_general(a, b, dims, preferred_element_type=F32)


def rows_of(i, size):
    return pl.ds(pl.multiple_of(i * size, size), size)


def attend_block(b, j, length, qin, gin, kbuf, ob, qs, gs, de, s_scr, p_scr):
    base = b * M
    mine = rows_of(b, M)

    def head(h):
        return pl.ds(pl.multiple_of(base + h * R, R), R)

    for h in range(G):
        qs[head(h), :] = qin[b, :, h * DH : (h + 1) * DH]
    q = qs[mine, :]

    def scores(k, m):
        s = dot(q, kbuf[0, k], NT)
        s_scr[k] = s
        for t in range(CH // 128):
            m = jnp.maximum(m, s[:, t * 128 : (t + 1) * 128])
        return m

    m = lax.fori_loop(0, b + 1, scores, jnp.full((M, 128), NEG, F32))
    last = b + 1
    s = dot(q, kbuf[0, last], NT)
    row = lax.broadcasted_iota(jnp.int32, (R, CH), 0) + j * R
    col = lax.broadcasted_iota(jnp.int32, (R, CH), 1)
    s = jnp.where(jnp.concatenate([col <= row] * G, axis=0), s, NEG)
    s_scr[last] = s
    for t in range(CH // 128):
        m = jnp.maximum(m, s[:, t * 128 : (t + 1) * 128])
    top = jnp.max(m, axis=1, keepdims=True) * CEXP

    def mix(k, carry):
        o, l = carry
        p = jnp.exp2(s_scr[k] * CEXP - top)
        for t in range(CH // 128):
            l = l + p[:, t * 128 : (t + 1) * 128]
        p = p.astype(BF)
        p_scr[k, mine, :] = p
        return o + dot(p, kbuf[1, k], NN), l

    o, l = lax.fori_loop(0, b + 2, mix, (jnp.zeros((M, DH), F32), jnp.zeros((M, 128), F32)))
    rl = 1.0 / jnp.sum(l, axis=1, keepdims=True)
    token = lax.broadcasted_iota(jnp.int32, (R, 1), 0) + (4 * b + j) * R
    valid = jnp.concatenate([token < length] * G, axis=0)
    o = jnp.where(valid, o * rl, 0.0).astype(BF)
    for h in range(G):
        ob[b, :, h * DH : (h + 1) * DH] = o[h * R : (h + 1) * R, :]
        gs[head(h), :] = gin[b, :, h * DH : (h + 1) * DH]
    gl = jnp.where(valid, gs[mine, :].astype(F32) * rl, 0.0).astype(BF)
    gs[mine, :] = gl
    delta = jnp.sum(gl.astype(F32) * o.astype(F32), axis=1, keepdims=True)
    de[mine, :] = jnp.broadcast_to(delta, (M, 128))


def grad_terms(k, rows, kbuf, qs, gs, de, p_scr, dka, dva, fresh):
    gl = gs[rows, :]
    delta = de[rows, :]
    p = p_scr[k, rows, :]
    dp = dot(gl, kbuf[1, k], NT)
    ds = jnp.concatenate(
        [
            (p[:, t : t + 128].astype(F32) * (dp[:, t : t + 128] - delta)).astype(BF)
            for t in range(0, CH, 128)
        ],
        axis=1,
    )
    dv = dot(p, gl, TN)
    dk = dot(ds, qs[rows, :], TN)
    dva[k] = dv if fresh else dva[k] + dv
    dka[k] = dk if fresh else dka[k] + dk
    return dot(ds, kbuf[0, k], NN)


def kernel(
    n,
    len_ref, q_ref, rk_ref, rv_ref, pk_ref, pv_ref, g_ref,
    out_ref, dq_ref, drk_ref, drv_ref, dpk_ref, dpv_ref,
    qin, gin, kbuf, ob, dqb, qs, gs, de, dqa, s_scr, p_scr, dka, dva,
    s1, r1, s2, r2, s3, ps, pin, pown, pall, len_s,
    loc, kv_send, kv_recv, qg_send, qg_recv, f_send, f_recv, o_send, o_recv,
    c_send, c_recv, x_send, x_recv, rs_send, rs_recv, ag_send, ag_recv, px_send, px_recv,
    fin,
):
    c = lax.axis_index("ctx")
    r = lax.axis_index("resp")
    x, j = c // 4, c % 4
    zl, core = j // 2, j % 2
    core_mate = x * 4 + zl * 2 + (1 - core)
    z_mate = x * 4 + (1 - zl) * 2 + core
    j_c = zl * 2 + (1 - core)
    j_z = (1 - zl) * 2 + core
    ORDER = (1, 3, 2)
    prow = 256 // n

    def other(d):
        return (x + d) % 4

    def source(d):
        return (x + 4 - d) % 4

    def send(src, dst, ssem, rsem, **where):
        return pltpu.make_async_remote_copy(
            src_ref=src, dst_ref=dst, send_sem=ssem, recv_sem=rsem,
            device_id=where, device_id_type=MESH,
        )

    barrier = pltpu.get_barrier_semaphore()
    for d in ORDER:
        pl.semaphore_signal(barrier, inc=1, device_id={"ctx": other(d) * 4 + j}, device_id_type=MESH)
    for mate in (core_mate, z_mate):
        pl.semaphore_signal(barrier, inc=1, device_id={"ctx": mate}, device_id_type=MESH)
    for e in range(1, n):
        pl.semaphore_signal(barrier, inc=1, device_id={"resp": (r + e) % n}, device_id_type=MESH)
    pl.semaphore_wait(barrier, 5 + n - 1)

    def head_cols(h):
        return rows_of(h, DH)

    def kv_pairs(h, at):
        cols = head_cols(h)
        rows = rows_of(j, R)
        prows = pl.ds(pl.multiple_of(j * R + at * PR, PR), PR)
        return (
            (rk_ref.at[0, :, cols], kbuf.at[0, 1 + at, rows, :]),
            (rv_ref.at[0, :, cols], kbuf.at[1, 1 + at, rows, :]),
            (pk_ref.at[:, cols], kbuf.at[0, 0, prows, :]),
            (pv_ref.at[:, cols], kbuf.at[1, 0, prows, :]),
        )

    len_copy = pltpu.make_async_copy(len_ref, len_s, fin.at[6])
    len_copy.start()
    kv_copies = {}
    for d in ORDER:
        kv_copies[d] = [
            send(src, dst, kv_send.at[d - 1, i], kv_recv.at[d - 1, i], ctx=other(d) * 4 + j)
            for i, (src, dst) in enumerate(kv_pairs(other(d), x))
        ]
        for cp in kv_copies[d]:
            cp.start()
    own = [pltpu.make_async_copy(src, dst, loc.at[i]) for i, (src, dst) in enumerate(kv_pairs(x, x))]
    for cp in own:
        cp.start()

    def qg_pairs(h, at):
        cols = rows_of(h, GW)
        return ((q_ref.at[0, :, cols], qin.at[at]), (g_ref.at[0, :, cols], gin.at[at]))

    qg_copies = []
    for d in ORDER:
        for i, (src, dst) in enumerate(qg_pairs(other(d), x)):
            cp = send(src, dst, qg_send.at[d, i], qg_recv.at[d, i], ctx=other(d) * 4 + j)
            cp.start()
            qg_copies.append(cp)
    for i, (src, dst) in enumerate(qg_pairs(x, x)):
        pltpu.make_async_copy(src, dst, qg_recv.at[0, i]).start()

    fwd = []

    def hand_on(slot, chunk, rows_j, kind, mate):
        view = kbuf.at[:, chunk, rows_of(rows_j, R), :]
        cp = send(view, view, f_send.at[slot, kind], f_recv.at[slot, kind], ctx=mate)
        cp.start()
        fwd.append(cp)

    def wait_handed(slot, chunk, rows_j, kind, mate):
        view = kbuf.at[:, chunk, rows_of(rows_j, R), :]
        send(view, view, f_send.at[slot, kind], f_recv.at[slot, kind], ctx=mate).wait_recv()

    for cp in own:
        cp.wait()
    hand_on(0, 1 + x, j, 0, core_mate)
    hand_on(0, 1 + x, j, 1, z_mate)
    for d in ORDER:
        for i, (src, dst) in enumerate(kv_pairs(x, source(d))):
            send(src, dst, kv_send.at[d - 1, i], kv_recv.at[d - 1, i], ctx=c).wait_recv()
        hand_on(d, 1 + source(d), j, 0, core_mate)
        hand_on(d, 1 + source(d), j, 1, z_mate)
    hand_on(4, 0, j, 0, core_mate)
    hand_on(4, 0, j, 1, z_mate)
    slots = [(0, 1 + x)] + [(d, 1 + source(d)) for d in ORDER] + [(4, 0)]
    for slot, chunk in slots:
        wait_handed(slot, chunk, j_z, 1, z_mate)
        hand_on(slot, chunk, j_z, 2, core_mate)
    for slot, chunk in slots:
        wait_handed(slot, chunk, j_c, 0, core_mate)
        wait_handed(slot, chunk, 3 - j, 2, core_mate)

    len_copy.wait()
    length = len_s[0]

    def result_pairs(b, h):
        cols = rows_of(h, GW)
        return ((ob.at[b], out_ref.at[0, :, cols]), (dqb.at[b], dq_ref.at[0, :, cols]))

    def part(k, kv, jj):
        rows = rows_of(jj, R)
        if kv == 0:
            return dka[k, rows, :] * SCALE
        return dva[k, rows, :]

    def to_core(k):
        return send(s1.at[k], r1.at[k], c_send.at[0, k], c_recv.at[0, k], ctx=core_mate)

    def to_z(k):
        return send(s2.at[k], r2.at[k], c_send.at[1, k], c_recv.at[1, k], ctx=z_mate)

    def row_pairs(at, h):
        cols = head_cols(h)
        return ((s3.at[at, 0], drk_ref.at[0, :, cols]), (s3.at[at, 1], drv_ref.at[0, :, cols]))

    def scatter(e, carry):
        to = (r + e) % n
        send(ps.at[rows_of(to, prow), :], pin.at[e], rs_send.at[e], rs_recv.at[e], resp=to).start()
        return carry

    def give_core(k):
        for kv in range(2):
            for zz in range(2):
                s1[k, zz, kv] = part(k, kv, 2 * zz + 1 - core).astype(BF)
        to_core(k).start()

    def give_z(k):
        to_core(k).wait_recv()
        for kv in range(2):
            s2[k, kv] = (part(k, kv, j_z) + r1[k, 1 - zl, kv].astype(F32)).astype(BF)
        to_z(k).start()

    def give_x(k):
        to_z(k).wait_recv()
        sums = [
            part(k, kv, j) + r1[k, zl, kv].astype(F32) + r2[k, kv].astype(F32) for kv in range(2)
        ]
        if k == 0:
            for kv in range(2):
                pown[kv * R : (kv + 1) * R, :] = sums[kv]
                ps[kv * R : (kv + 1) * R, :] = sums[kv].astype(BF)
            lax.fori_loop(1, n, scatter, 0)
            return
        at = k - 1
        for kv in range(2):
            s3[at, kv] = sums[kv].astype(BF)

        @pl.when(x == at)
        def _():
            for t, (src, dst) in enumerate(row_pairs(at, x)):
                pltpu.make_async_copy(src, dst, fin.at[2 + t]).start()

        @pl.when(x != at)
        def _():
            d = (at + 4 - x) % 4
            for t, (src, dst) in enumerate(row_pairs(at, x)):
                send(src, dst, x_send.at[d, t], x_recv.at[d, t], ctx=at * 4 + j).start()

    def gather_sum(e, acc):
        send(ps.at[rows_of(r, prow), :], pin.at[e], rs_send.at[e], rs_recv.at[e], resp=r).wait_recv()
        return acc + pin[e].astype(F32)

    def spread(e, carry):
        to = (r + e) % n
        view = pall.at[rows_of(r, prow), :]
        send(view, view, ag_send.at[e], ag_recv.at[e], resp=to).start()
        return carry

    def sum_prompt():
        psum = lax.fori_loop(1, n, gather_sum, pown[rows_of(r, prow), :])
        pall[rows_of(r, prow), :] = psum.astype(BF)
        lax.fori_loop(1, n, spread, 0)

    def step(i, carry):
        d = jnp.where(i == 0, 0, jnp.where(i == 1, 1, jnp.where(i == 2, 3, 2)))
        b = (x + 4 - d) % 4
        for t, (src, dst) in enumerate(qg_pairs(x, b)):
            pltpu.make_async_copy(src, dst, qg_recv.at[d, t]).wait()
        attend_block(b, j, length, qin, gin, kbuf, ob, qs, gs, de, s_scr, p_scr)
        src, dst = result_pairs(b, x)[0]

        @pl.when(i == 0)
        def _():
            pltpu.make_async_copy(src, dst, fin.at[0]).start()

        @pl.when(i > 0)
        def _():
            send(src, dst, o_send.at[d, 0], o_recv.at[d, 0], ctx=b * 4 + j).start()

        return carry

    lax.fori_loop(0, 4, step, 0)

    def chunk_terms(k, low, fresh_dq):
        for b in range(low, 4):
            rows = slice(b * M, (b + 1) * M)
            dq = grad_terms(k, rows, kbuf, qs, gs, de, p_scr, dka, dva, b == low)
            dqa[rows, :] = dq if fresh_dq else dqa[rows, :] + dq

    chunk_terms(0, 0, True)
    give_core(0)
    chunk_terms(4, 3, False)
    give_core(4)
    give_z(0)
    chunk_terms(3, 2, False)
    give_core(3)
    give_z(4)
    give_x(0)
    chunk_terms(2, 1, False)
    give_core(2)
    give_z(3)
    give_x(4)
    sum_prompt()
    for u, d in enumerate((2, 1, 3, 0)):
        b = source(d)
        rows = rows_of(b, M)
        dq = grad_terms(1, rows, kbuf, qs, gs, de, p_scr, dka, dva, u == 0)
        dq = ((dqa[rows, :] + dq) * SCALE).astype(BF)
        for h in range(G):
            dqb[b, :, h * DH : (h + 1) * DH] = dq[h * R : (h + 1) * R, :]
        src, dst = result_pairs(b, x)[1]
        if d:
            send(src, dst, o_send.at[d, 1], o_recv.at[d, 1], ctx=b * 4 + j).start()
        else:
            pltpu.make_async_copy(src, dst, fin.at[1]).start()
        if u == 1:
            give_z(2)
            give_x(3)
    give_core(1)
    give_x(2)
    give_z(1)
    finals = [pltpu.make_async_copy(src, dst, fin.at[t]) for t, (src, dst) in enumerate(result_pairs(x, x))]

    def collect(e, carry):
        view = pall.at[rows_of((r + n - e) % n, prow), :]
        send(view, view, ag_send.at[e], ag_recv.at[e], resp=r).wait_recv()
        return carry

    lax.fori_loop(1, n, collect, 0)

    def prompt_pairs(at, h):
        cols = head_cols(h)
        return (
            (pall.at[rows_of(at, PR), :], dpk_ref.at[:, cols]),
            (pall.at[rows_of(4 + at, PR), :], dpv_ref.at[:, cols]),
        )

    px_copies = []
    for d in ORDER:
        for t, (src, dst) in enumerate(prompt_pairs(other(d), x)):
            cp = send(src, dst, px_send.at[d, t], px_recv.at[d, t], ctx=other(d) * 4 + j)
            cp.start()
            px_copies.append(cp)
    for t, (src, dst) in enumerate(prompt_pairs(x, x)):
        cp = pltpu.make_async_copy(src, dst, fin.at[4 + t])
        cp.start()
        finals.append(cp)
    give_x(1)
    for t, (src, dst) in enumerate(row_pairs(x, x)):
        finals.append(pltpu.make_async_copy(src, dst, fin.at[2 + t]))

    for d in ORDER:
        for t in range(2):
            src, dst = result_pairs(source(d), other(d))[t]
            cp = send(src, dst, o_send.at[d, t], o_recv.at[d, t], ctx=source(d) * 4 + j)
            cp.wait_recv()
            cp.wait_send()
            src, dst = row_pairs(x, source(d))[t]
            cp = send(src, dst, x_send.at[d, t], x_recv.at[d, t], ctx=c)
            cp.wait_recv()
            cp.wait_send()
            src, dst = prompt_pairs(x, source(d))[t]
            send(src, dst, px_send.at[d, t], px_recv.at[d, t], ctx=c).wait_recv()
    for cp in finals:
        cp.wait()
    for d in ORDER:
        for cp in kv_copies[d]:
            cp.wait_send()
    for cp in qg_copies + fwd + px_copies:
        cp.wait_send()
    for k in range(NC):
        to_core(k).wait_send()
        to_z(k).wait_send()

    def sent(e, carry):
        send(ps.at[rows_of(r, prow), :], pin.at[e], rs_send.at[e], rs_recv.at[e], resp=r).wait_send()
        view = pall.at[rows_of(r, prow), :]
        send(view, view, ag_send.at[e], ag_recv.at[e], resp=r).wait_send()
        return carry

    lax.fori_loop(1, n, sent, 0)


def finish(*refs):
    ins, outs, sems = refs[:6], refs[6:12], refs[12]
    copies = [pltpu.make_async_copy(src, dst, sems.at[i]) for i, (src, dst) in enumerate(zip(ins, outs))]
    for cp in copies:
        cp.start()
    for cp in copies:
        cp.wait()


def body(n, queries, resp_keys, resp_values, prompt_keys, prompt_values, out_grad, lengths):
    shape = jax.ShapeDtypeStruct
    anywhere = pl.BlockSpec(memory_space=pl.ANY)
    vmem = pltpu.VMEM
    dma = pltpu.SemaphoreType.DMA
    outs = (
        shape((1, R, HQ * DH), BF),
        shape((1, R, HQ * DH), BF),
        shape((1, R, HK * DH), BF),
        shape((1, R, HK * DH), BF),
        shape((PR, HK * DH), BF),
        shape((PR, HK * DH), BF),
    )
    results = pl.pallas_call(
        functools.partial(kernel, n),
        out_shape=outs,
        in_specs=[anywhere] * 7,
        out_specs=(anywhere,) * 6,
        scratch_shapes=[
            vmem((4, R, GW), BF), vmem((4, R, GW), BF), vmem((2, NC, CH, DH), BF),
            vmem((4, R, GW), BF), vmem((4, R, GW), BF), vmem((4 * M, DH), BF), vmem((4 * M, DH), BF),
            vmem((4 * M, 128), F32), vmem((4 * M, DH), F32),
            vmem((NC, M, CH), F32), vmem((NC, 4 * M, CH), BF), vmem((NC, CH, DH), F32), vmem((NC, CH, DH), F32),
            vmem((NC, 2, 2, R, DH), BF), vmem((NC, 2, 2, R, DH), BF),
            vmem((NC, 2, R, DH), BF), vmem((NC, 2, R, DH), BF), vmem((4, 2, R, DH), BF),
            vmem((2 * R, DH), BF), vmem((n, 256 // n, DH), BF), vmem((2 * R, DH), F32), vmem((2 * R, DH), BF),
            pltpu.SMEM((1,), jnp.int32),
            dma((4,)), dma((3, 4)), dma((3, 4)), dma((4, 2)), dma((4, 2)), dma((5, 3)), dma((5, 3)),
            dma((4, 2)), dma((4, 2)), dma((2, NC)), dma((2, NC)), dma((4, 2)), dma((4, 2)),
            dma((n,)), dma((n,)), dma((n,)), dma((n,)), dma((4, 2)), dma((4, 2)), dma((7,)),
        ],
        compiler_params=pltpu.CompilerParams(
            collective_id=0, has_side_effects=True, vmem_limit_bytes=56 << 20
        ),
    )(lengths, queries, resp_keys, resp_values, prompt_keys, prompt_values, out_grad)
    return pl.pallas_call(
        finish,
        out_shape=outs,
        in_specs=[pl.BlockSpec(memory_space=vmem)] * 6,
        out_specs=(anywhere,) * 6,
        scratch_shapes=[dma((6,))],
    )(*results)


def solution(mesh):
    seq = P("resp", "ctx", None)
    return jax.shard_map(
        functools.partial(body, mesh.shape["resp"]),
        mesh=mesh,
        in_specs=(seq, seq, seq, P("ctx", None), P("ctx", None), seq, P("resp")),
        out_specs=(seq, seq, seq, seq, P("ctx", None), P("ctx", None)),
        check_vma=False,
    )
```

```python
import functools
import math

import jax
import jax.numpy as jnp
from jax import lax
from jax.experimental import pallas as pl
from jax.experimental.pallas import tpu as pltpu
from jax.sharding import PartitionSpec as P

DH = 128
HQ = 20
HK = 4
G = HQ // HK
GW = G * DH
R = 128
M = G * R
CH = 512
NC = 5
PR = 32
BF = jnp.bfloat16
F32 = jnp.float32
MESH = pl.DeviceIdType.MESH
SCALE = DH**-0.5
CEXP = SCALE * math.log2(math.e)
NEG = -1e30
NT = (((1,), (1,)), ((), ()))
NN = (((1,), (0,)), ((), ()))
TN = (((0,), (0,)), ((), ()))


def dot(a, b, dims):
    return lax.dot_general(a, b, dims, preferred_element_type=F32)


def rows_of(i, size):
    return pl.ds(pl.multiple_of(i * size, size), size)


def attend_block(b, j, length, qin, gin, kbuf, ob, qs, gs, de, s_scr, p_scr):
    base = b * M
    mine = slice(base, base + M)
    last = b + 1
    for h in range(G):
        qs[base + h * R : base + (h + 1) * R, :] = qin[b, :, h * DH : (h + 1) * DH]
    q = qs[mine, :]
    row = lax.broadcasted_iota(jnp.int32, (R, 128), 0) + j * R
    col = lax.broadcasted_iota(jnp.int32, (R, 128), 1)
    m = jnp.full((M, 128), NEG, F32)
    for k in range(last + 1):
        s = dot(q, kbuf[0, k], NT)
        for t in range(0, CH, 128):
            part = s[:, t : t + 128]
            if k == last:
                part = jnp.where(jnp.concatenate([col + t <= row] * G, axis=0), part, NEG)
            s_scr[k, :, t : t + 128] = part
            m = jnp.maximum(m, part)
    top = jnp.broadcast_to(jnp.max(m, axis=1, keepdims=True) * CEXP, (M, 128))
    o = jnp.zeros((M, DH), F32)
    l = jnp.zeros((M, 128), F32)
    for k in range(last + 1):
        ps = []
        for t in range(0, CH, 128):
            p = jnp.exp2(s_scr[k, :, t : t + 128] * CEXP - top)
            l = l + p
            ps.append(p.astype(BF))
        p = jnp.concatenate(ps, axis=1)
        p_scr[k, mine, :] = p
        o = o + dot(p, kbuf[1, k], NN)
    rl = 1.0 / jnp.sum(l, axis=1, keepdims=True)
    token = lax.broadcasted_iota(jnp.int32, (R, 1), 0) + (4 * b + j) * R
    valid = jnp.concatenate([token < length] * G, axis=0)
    o = jnp.where(valid, o * rl, 0.0).astype(BF)
    for h in range(G):
        ob[b, :, h * DH : (h + 1) * DH] = o[h * R : (h + 1) * R, :]
        gs[base + h * R : base + (h + 1) * R, :] = gin[b, :, h * DH : (h + 1) * DH]
    gl = jnp.where(valid, gs[mine, :].astype(F32) * rl, 0.0).astype(BF)
    gs[mine, :] = gl
    delta = jnp.sum(gl.astype(F32) * o.astype(F32), axis=1, keepdims=True)
    de[mine, :] = jnp.broadcast_to(delta, (M, 128))


def grad_terms(k, rows, kbuf, qs, gs, de, p_scr, dka, dva):
    gl = gs[rows, :]
    delta = de[rows, :]
    p = p_scr[k, rows, :]
    dp = dot(gl, kbuf[1, k], NT)
    ds = jnp.concatenate(
        [
            (p[:, t : t + 128].astype(F32) * (dp[:, t : t + 128] - delta)).astype(BF)
            for t in range(0, CH, 128)
        ],
        axis=1,
    )
    dva[k] += dot(p, gl, TN)
    dka[k] += dot(ds, qs[rows, :], TN)
    return dot(ds, kbuf[0, k], NN)


def kernel(
    n,
    len_ref, q_ref, rk_ref, rv_ref, pk_ref, pv_ref, g_ref,
    out_ref, dq_ref, drk_ref, drv_ref, dpk_ref, dpv_ref,
    qin, gin, kbuf, ob, dqb, qs, gs, de, dqa, s_scr, p_scr, dka, dva,
    s1, r1, s2, r2, s3, ps, pin, pown, pall, pfin, len_s,
    loc, kv_send, kv_recv, qg_send, qg_recv, f_send, f_recv, o_send, o_recv,
    c_send, c_recv, x_send, x_recv, rs_send, rs_recv, ag_send, ag_recv,
    fin, lead_sem, go_sem,
):
    c = lax.axis_index("ctx")
    r = lax.axis_index("resp")
    x, j = c // 4, c % 4
    zl, core = j // 2, j % 2
    core_mate = x * 4 + zl * 2 + (1 - core)
    z_mate = x * 4 + (1 - zl) * 2 + core
    j_c = zl * 2 + (1 - core)
    j_z = (1 - zl) * 2 + core
    ORDER = (1, 3, 2)
    prow = 256 // n

    def other(d):
        return (x + d) % 4

    def source(d):
        return (x + 4 - d) % 4

    def send(src, dst, ssem, rsem, **where):
        return pltpu.make_async_remote_copy(
            src_ref=src, dst_ref=dst, send_sem=ssem, recv_sem=rsem,
            device_id=where, device_id_type=MESH,
        )

    barrier = pltpu.get_barrier_semaphore()
    leader = c == 0
    near = [other(d) * 4 + j for d in ORDER] + [core_mate, z_mate]
    for to in near:

        @pl.when(to != 0)
        def _():
            pl.semaphore_signal(barrier, inc=1, device_id={"ctx": to}, device_id_type=MESH)

    by_leader = jnp.logical_or(j == 0, jnp.logical_and(x == 0, j < 3))

    @pl.when(jnp.logical_not(leader))
    def _():
        pl.semaphore_wait(barrier, 5)

        @pl.when(by_leader)
        def _():
            pl.semaphore_signal(lead_sem, inc=1, device_id={"ctx": 0}, device_id_type=MESH)

    @pl.when(leader)
    def _():
        pl.semaphore_wait(lead_sem, 5)

    def head_cols(h):
        return rows_of(h, DH)

    def kv_pairs(h, at):
        cols = head_cols(h)
        rows = rows_of(j, R)
        prows = pl.ds(pl.multiple_of(j * R + at * PR, PR), PR)
        return (
            (rk_ref.at[0, :, cols], kbuf.at[0, 1 + at, rows, :]),
            (rv_ref.at[0, :, cols], kbuf.at[1, 1 + at, rows, :]),
            (pk_ref.at[:, cols], kbuf.at[0, 0, prows, :]),
            (pv_ref.at[:, cols], kbuf.at[1, 0, prows, :]),
        )

    len_copy = pltpu.make_async_copy(len_ref, len_s, fin.at[6])
    len_copy.start()
    kv_copies = {}
    for d in ORDER:
        kv_copies[d] = [
            send(src, dst, kv_send.at[d - 1, i], kv_recv.at[d - 1, i], ctx=other(d) * 4 + j)
            for i, (src, dst) in enumerate(kv_pairs(other(d), x))
        ]
        for cp in kv_copies[d]:
            cp.start()
    own = [pltpu.make_async_copy(src, dst, loc.at[i]) for i, (src, dst) in enumerate(kv_pairs(x, x))]
    for cp in own:
        cp.start()

    def qg_pairs(h, at):
        cols = rows_of(h, GW)
        return ((q_ref.at[0, :, cols], qin.at[at]), (g_ref.at[0, :, cols], gin.at[at]))

    qg_copies = []
    for d in ORDER:
        for i, (src, dst) in enumerate(qg_pairs(other(d), x)):
            cp = send(src, dst, qg_send.at[d, i], qg_recv.at[d, i], ctx=other(d) * 4 + j)
            cp.start()
            qg_copies.append(cp)
    for i, (src, dst) in enumerate(qg_pairs(x, x)):
        pltpu.make_async_copy(src, dst, qg_recv.at[0, i]).start()

    fwd = []

    def hand_on(slot, chunk, rows_j, kind, mate):
        view = kbuf.at[:, chunk, rows_of(rows_j, R), :]
        cp = send(view, view, f_send.at[slot, kind], f_recv.at[slot, kind], ctx=mate)
        cp.start()
        fwd.append(cp)

    def wait_handed(slot, chunk, rows_j, kind, mate):
        view = kbuf.at[:, chunk, rows_of(rows_j, R), :]
        send(view, view, f_send.at[slot, kind], f_recv.at[slot, kind], ctx=mate).wait_recv()

    for cp in own:
        cp.wait()
    hand_on(0, 1 + x, j, 0, core_mate)
    hand_on(0, 1 + x, j, 1, z_mate)
    for d in ORDER:
        for i, (src, dst) in enumerate(kv_pairs(x, source(d))):
            send(src, dst, kv_send.at[d - 1, i], kv_recv.at[d - 1, i], ctx=c).wait_recv()
        hand_on(d, 1 + source(d), j, 0, core_mate)
        hand_on(d, 1 + source(d), j, 1, z_mate)
    hand_on(4, 0, j, 0, core_mate)
    hand_on(4, 0, j, 1, z_mate)
    slots = [(0, 1 + x)] + [(d, 1 + source(d)) for d in ORDER] + [(4, 0)]
    dka[...] = jnp.zeros_like(dka)
    dva[...] = jnp.zeros_like(dva)
    for slot, chunk in slots:
        wait_handed(slot, chunk, j_z, 1, z_mate)
        hand_on(slot, chunk, j_z, 2, core_mate)
    for slot, chunk in slots:
        wait_handed(slot, chunk, j_c, 0, core_mate)
        wait_handed(slot, chunk, 3 - j, 2, core_mate)

    @pl.when(leader)
    def _():
        for e in range(1, n):
            pl.semaphore_signal(barrier, inc=1, device_id={"resp": (r + e) % n}, device_id_type=MESH)

    def meet_responses():
        @pl.when(leader)
        def _():
            pl.semaphore_wait(barrier, n - 1)
            for to in range(1, 16):
                pl.semaphore_signal(go_sem, inc=1, device_id={"ctx": to}, device_id_type=MESH)

        @pl.when(jnp.logical_not(leader))
        def _():
            pl.semaphore_wait(go_sem, 1)

    len_copy.wait()
    length = len_s[0]

    def result_pairs(b, h):
        cols = rows_of(h, GW)
        return ((ob.at[b], out_ref.at[0, :, cols]), (dqb.at[b], dq_ref.at[0, :, cols]))

    def part(k, kv, jj):
        rows = rows_of(jj, R)
        if kv == 0:
            return dka[k, rows, :] * SCALE
        return dva[k, rows, :]

    def to_core(k):
        return send(s1.at[k], r1.at[k], c_send.at[0, k], c_recv.at[0, k], ctx=core_mate)

    def to_z(k):
        return send(s2.at[k], r2.at[k], c_send.at[1, k], c_recv.at[1, k], ctx=z_mate)

    def row_pairs(at, h):
        cols = head_cols(h)
        return ((s3.at[at, 0], drk_ref.at[0, :, cols]), (s3.at[at, 1], drv_ref.at[0, :, cols]))

    def scatter(e, carry):
        to = (r + e) % n
        send(ps.at[rows_of(to, prow), :], pin.at[e], rs_send.at[e], rs_recv.at[e], resp=to).start()
        return carry

    def give_core(k):
        for kv in range(2):
            for zz in range(2):
                s1[k, zz, kv] = part(k, kv, 2 * zz + 1 - core).astype(BF)
        to_core(k).start()

    def give_z(k):
        to_core(k).wait_recv()
        for kv in range(2):
            s2[k, kv] = (part(k, kv, j_z) + r1[k, 1 - zl, kv].astype(F32)).astype(BF)
        to_z(k).start()

    def total(k, kv):
        return part(k, kv, j) + r1[k, zl, kv].astype(F32) + r2[k, kv].astype(F32)

    def give_prompt():
        to_z(0).wait_recv()
        for kv in range(2):
            t = total(0, kv)
            pown[kv * R : (kv + 1) * R, :] = t
            ps[kv * R : (kv + 1) * R, :] = t.astype(BF)
        meet_responses()
        lax.fori_loop(1, n, scatter, 0)

    def give_x(k):
        to_z(k).wait_recv()
        at = k - 1
        for kv in range(2):
            s3[at, kv] = total(k, kv).astype(BF)

        @pl.when(at == x)
        def _():
            for t, (src, dst) in enumerate(row_pairs(at, x)):
                pltpu.make_async_copy(src, dst, fin.at[2 + t]).start()

        @pl.when(at != x)
        def _():
            d = (at + 4 - x) % 4
            for t, (src, dst) in enumerate(row_pairs(at, x)):
                send(src, dst, x_send.at[d, t], x_recv.at[d, t], ctx=at * 4 + j).start()

    def over(fn, low, high):
        lax.fori_loop(low, high, lambda k, carry: (fn(k), carry)[1], 0)

    def gather_sum(e, acc):
        send(ps.at[rows_of(r, prow), :], pin.at[e], rs_send.at[e], rs_recv.at[e], resp=r).wait_recv()
        return acc + pin[e].astype(F32)

    brows = min(PR, prow)
    nblk = prow // brows
    per_x = PR // brows

    def piece(t):
        g = r * nblk + t
        kv, rest = g // (4 * per_x), g % (4 * per_x)
        return kv, rest // per_x, rest % per_x

    def piece_copy(e, t):
        kv, at, half = piece(t)
        src = pall.at[rows_of(r * nblk + t, brows), :]
        dst = pfin.at[kv, rows_of(half, brows), head_cols(x)]
        rsem = ag_recv.at[kv * per_x + half, x]
        away = send(src, dst, ag_send.at[e, t], rsem, resp=(r + e) % n, ctx=at * 4 + j)
        home = pltpu.make_async_copy(src, dst, rsem)
        return away, home, jnp.logical_and(e == 0, at == x)

    def spread(e, carry):
        for t in range(nblk):
            away, home, here = piece_copy(e, t)
            pl.when(here)(home.start)
            pl.when(jnp.logical_not(here))(away.start)
        return carry

    def spread_sent(e, carry):
        for t in range(nblk):
            away, home, here = piece_copy(e, t)
            pl.when(jnp.logical_not(here))(away.wait_send)
        return carry

    def collect(i, carry):
        kv, rest = i // (4 * per_x), i % (4 * per_x)
        half, h = rest // 4, rest % 4
        dst = pfin.at[kv, rows_of(half, brows), head_cols(h)]
        src = pall.at[rows_of(0, brows), :]
        pltpu.make_async_copy(src, dst, ag_recv.at[kv * per_x + half, h]).wait()
        return carry

    def sum_prompt():
        psum = lax.fori_loop(1, n, gather_sum, pown[rows_of(r, prow), :])
        pall[rows_of(r, prow), :] = psum.astype(BF)
        lax.fori_loop(0, n, spread, 0)

    def step(i, carry):
        d = jnp.where(i == 0, 0, jnp.where(i == 1, 1, jnp.where(i == 2, 3, 2)))
        b = (x + 4 - d) % 4
        for t, (src, dst) in enumerate(qg_pairs(x, b)):
            pltpu.make_async_copy(src, dst, qg_recv.at[d, t]).wait()
        for bb in range(4):

            @pl.when(b == bb)
            def _():
                attend_block(bb, j, length, qin, gin, kbuf, ob, qs, gs, de, s_scr, p_scr)

        src, dst = result_pairs(b, x)[0]

        @pl.when(i == 0)
        def _():
            pltpu.make_async_copy(src, dst, fin.at[0]).start()

        @pl.when(i > 0)
        def _():
            send(src, dst, o_send.at[d, 0], o_recv.at[d, 0], ctx=b * 4 + j).start()

        return carry

    lax.fori_loop(0, 4, step, 0)

    def terms(k, rows):
        return grad_terms(k, rows, kbuf, qs, gs, de, p_scr, dka, dva)

    for b in range(4):
        rows = slice(b * M, (b + 1) * M)
        dqa[rows, :] = terms(0, rows)
    give_core(0)

    ends = []
    for d in (2, 1, 3):
        ends.append((ends[-1] if ends else 0) + source(d) + 1)

    def unit(u, carry):
        past = [u >= end for end in ends]
        d = jnp.where(past[2], 0, jnp.where(past[1], 3, jnp.where(past[0], 1, 2)))
        begin = jnp.where(past[2], ends[2], jnp.where(past[1], ends[1], jnp.where(past[0], ends[0], 0)))
        b = (x + 4 - d) % 4
        k = u - begin + 1
        rows = rows_of(b, M)
        dqa[rows, :] += terms(k, rows)
        own = d == 0

        @pl.when(own)
        def _():
            give_core(k)

        @pl.when(k == b + 1)
        def _():
            for h in range(G):
                dq = dqa[pl.ds(pl.multiple_of(b * M + h * R, R), R), :]
                dqb[b, :, h * DH : (h + 1) * DH] = (dq * SCALE).astype(BF)
            src, dst = result_pairs(b, x)[1]

            @pl.when(own)
            def _():
                pltpu.make_async_copy(src, dst, fin.at[1]).start()

            @pl.when(jnp.logical_not(own))
            def _():
                send(src, dst, o_send.at[d, 1], o_recv.at[d, 1], ctx=b * 4 + j).start()

        @pl.when(u == 1)
        def _():
            give_z(0)

        @pl.when(u == 4)
        def _():
            give_prompt()

        @pl.when(u + 1 == ends[2])
        def _():
            over(give_core, x + 2, NC)

        @pl.when(jnp.logical_and(own, k == 1))
        def _():
            over(give_z, x + 2, NC)

        @pl.when(jnp.logical_and(own, k >= 2))
        def _():
            give_z(k - 1)

        @pl.when(jnp.logical_and(own, k == 3))
        def _():
            over(give_x, x + 2, NC)

        @pl.when(jnp.logical_and(own, k >= 3))
        def _():
            give_x(k - 2)

        @pl.when(u == 8)
        def _():
            sum_prompt()

        return carry

    lax.fori_loop(0, 10, unit, 0)
    give_z(x + 1)

    @pl.when(x < 2)
    def _():
        over(give_x, x + 2, NC)

    over(give_x, jnp.maximum(x, 1), x + 2)
    finals = [pltpu.make_async_copy(src, dst, fin.at[t]) for t, (src, dst) in enumerate(result_pairs(x, x))]
    lax.fori_loop(0, 8 * per_x, collect, 0)
    for kv, dst in enumerate((dpk_ref, dpv_ref)):
        cp = pltpu.make_async_copy(pfin.at[kv], dst, fin.at[4 + kv])
        cp.start()
        finals.append(cp)
    for t, (src, dst) in enumerate(row_pairs(x, x)):
        finals.append(pltpu.make_async_copy(src, dst, fin.at[2 + t]))

    for d in ORDER:
        for t in range(2):
            src, dst = result_pairs(source(d), other(d))[t]
            cp = send(src, dst, o_send.at[d, t], o_recv.at[d, t], ctx=source(d) * 4 + j)
            cp.wait_recv()
            cp.wait_send()
            src, dst = row_pairs(x, source(d))[t]
            cp = send(src, dst, x_send.at[d, t], x_recv.at[d, t], ctx=c)
            cp.wait_recv()
            cp.wait_send()
    for cp in finals:
        cp.wait()
    for d in ORDER:
        for cp in kv_copies[d]:
            cp.wait_send()
    for cp in qg_copies + fwd:
        cp.wait_send()
    for k in range(NC):
        to_core(k).wait_send()
        to_z(k).wait_send()

    def sent(e, carry):
        send(ps.at[rows_of(r, prow), :], pin.at[e], rs_send.at[e], rs_recv.at[e], resp=r).wait_send()
        return carry

    lax.fori_loop(1, n, sent, 0)
    lax.fori_loop(0, n, spread_sent, 0)


def finish(*refs):
    ins, outs, sems = refs[:6], refs[6:12], refs[12]
    copies = [pltpu.make_async_copy(src, dst, sems.at[i]) for i, (src, dst) in enumerate(zip(ins, outs))]
    for cp in copies:
        cp.start()
    for cp in copies:
        cp.wait()


def body(n, queries, resp_keys, resp_values, prompt_keys, prompt_values, out_grad, lengths):
    shape = jax.ShapeDtypeStruct
    anywhere = pl.BlockSpec(memory_space=pl.ANY)
    vmem = pltpu.VMEM
    dma = pltpu.SemaphoreType.DMA
    outs = (
        shape((1, R, HQ * DH), BF),
        shape((1, R, HQ * DH), BF),
        shape((1, R, HK * DH), BF),
        shape((1, R, HK * DH), BF),
        shape((PR, HK * DH), BF),
        shape((PR, HK * DH), BF),
    )
    results = pl.pallas_call(
        functools.partial(kernel, n),
        out_shape=outs,
        in_specs=[anywhere] * 7,
        out_specs=(anywhere,) * 6,
        scratch_shapes=[
            vmem((4, R, GW), BF), vmem((4, R, GW), BF), vmem((2, NC, CH, DH), BF),
            vmem((4, R, GW), BF), vmem((4, R, GW), BF), vmem((4 * M, DH), BF), vmem((4 * M, DH), BF),
            vmem((4 * M, 128), F32), vmem((4 * M, DH), F32),
            vmem((NC, M, CH), F32), vmem((NC, 4 * M, CH), BF), vmem((NC, CH, DH), F32), vmem((NC, CH, DH), F32),
            vmem((NC, 2, 2, R, DH), BF), vmem((NC, 2, 2, R, DH), BF),
            vmem((NC, 2, R, DH), BF), vmem((NC, 2, R, DH), BF), vmem((4, 2, R, DH), BF),
            vmem((2 * R, DH), BF), vmem((n, 256 // n, DH), BF), vmem((2 * R, DH), F32), vmem((2 * R, DH), BF),
            vmem((2, PR, HK * DH), BF),
            pltpu.SMEM((1,), jnp.int32),
            dma((4,)), dma((3, 4)), dma((3, 4)), dma((4, 2)), dma((4, 2)), dma((5, 3)), dma((5, 3)),
            dma((4, 2)), dma((4, 2)), dma((2, NC)), dma((2, NC)), dma((4, 2)), dma((4, 2)),
            dma((n,)), dma((n,)), dma((n, max(1, 8 // n))), dma((2 * max(1, n // 8), 4)), dma((7,)),
            pltpu.SemaphoreType.REGULAR, pltpu.SemaphoreType.REGULAR,
        ],
        compiler_params=pltpu.CompilerParams(
            collective_id=0, has_side_effects=True, vmem_limit_bytes=56 << 20
        ),
    )(lengths, queries, resp_keys, resp_values, prompt_keys, prompt_values, out_grad)
    return pl.pallas_call(
        finish,
        out_shape=outs,
        in_specs=[pl.BlockSpec(memory_space=vmem)] * 6,
        out_specs=(anywhere,) * 6,
        scratch_shapes=[dma((6,))],
    )(*results)


def solution(mesh):
    seq = P("resp", "ctx", None)
    return jax.shard_map(
        functools.partial(body, mesh.shape["resp"]),
        mesh=mesh,
        in_specs=(seq, seq, seq, P("ctx", None), P("ctx", None), seq, P("resp")),
        out_specs=(seq, seq, seq, seq, P("ctx", None), P("ctx", None)),
        check_vma=False,
    )
```

```python
import functools
import math

import jax
import jax.numpy as jnp
from jax import lax
from jax.experimental import pallas as pl
from jax.experimental.pallas import tpu as pltpu
from jax.sharding import PartitionSpec as P

DH = 128
HQ = 20
HK = 4
G = HQ // HK
GW = G * DH
R = 128
M = G * R
CH = 512
NC = 5
PR = 32
BF = jnp.bfloat16
F32 = jnp.float32
MESH = pl.DeviceIdType.MESH
SCALE = DH**-0.5
CEXP = SCALE * math.log2(math.e)
NEG = -1e30
NT = (((1,), (1,)), ((), ()))
NN = (((1,), (0,)), ((), ()))
TN = (((0,), (0,)), ((), ()))


def dot(a, b, dims):
    return lax.dot_general(a, b, dims, preferred_element_type=F32)


def rows_of(i, size):
    return pl.ds(pl.multiple_of(i * size, size), size)


def attend_block(b, j, length, qin, gin, kbuf, ob, qs, gs, de, s_scr, p_scr):
    base = b * M
    mine = slice(base, base + M)
    last = b + 1
    for h in range(G):
        qs[base + h * R : base + (h + 1) * R, :] = qin[b, :, h * DH : (h + 1) * DH]
    q = qs[mine, :]
    row = lax.broadcasted_iota(jnp.int32, (R, 128), 0) + j * R
    col = lax.broadcasted_iota(jnp.int32, (R, 128), 1)
    m = jnp.full((M, 128), NEG, F32)
    for k in range(last + 1):
        s = dot(q, kbuf[0, k], NT)
        for t in range(0, CH, 128):
            part = s[:, t : t + 128]
            if k == last:
                part = jnp.where(jnp.concatenate([col + t <= row] * G, axis=0), part, NEG)
            s_scr[k, :, t : t + 128] = part
            m = jnp.maximum(m, part)
    top = jnp.broadcast_to(jnp.max(m, axis=1, keepdims=True) * CEXP, (M, 128))
    o = jnp.zeros((M, DH), F32)
    l = jnp.zeros((M, 128), F32)
    for k in range(last + 1):
        ps = []
        for t in range(0, CH, 128):
            p = jnp.exp2(s_scr[k, :, t : t + 128] * CEXP - top)
            l = l + p
            ps.append(p.astype(BF))
        p = jnp.concatenate(ps, axis=1)
        p_scr[k, mine, :] = p
        o = o + dot(p, kbuf[1, k], NN)
    rl = 1.0 / jnp.sum(l, axis=1, keepdims=True)
    token = lax.broadcasted_iota(jnp.int32, (R, 1), 0) + (4 * b + j) * R
    valid = jnp.concatenate([token < length] * G, axis=0)
    o = jnp.where(valid, o * rl, 0.0).astype(BF)
    for h in range(G):
        ob[b, :, h * DH : (h + 1) * DH] = o[h * R : (h + 1) * R, :]
        gs[base + h * R : base + (h + 1) * R, :] = gin[b, :, h * DH : (h + 1) * DH]
    gl = jnp.where(valid, gs[mine, :].astype(F32) * rl, 0.0).astype(BF)
    gs[mine, :] = gl
    delta = jnp.sum(gl.astype(F32) * o.astype(F32), axis=1, keepdims=True)
    de[mine, :] = jnp.broadcast_to(delta, (M, 128))


def grad_terms(k, rows, kbuf, qs, gs, de, p_scr, dka, dva):
    gl = gs[rows, :]
    delta = de[rows, :]
    p = p_scr[k, rows, :]
    dp = dot(gl, kbuf[1, k], NT)
    ds = jnp.concatenate(
        [
            (p[:, t : t + 128].astype(F32) * (dp[:, t : t + 128] - delta)).astype(BF)
            for t in range(0, CH, 128)
        ],
        axis=1,
    )
    dva[k] += dot(p, gl, TN)
    dka[k] += dot(ds, qs[rows, :], TN)
    return dot(ds, kbuf[0, k], NN)


def kernel(
    n,
    len_ref, q_ref, rk_ref, rv_ref, pk_ref, pv_ref, g_ref,
    out_ref, dq_ref, drk_ref, drv_ref, dpk_ref, dpv_ref,
    qin, gin, kbuf, ob, dqb, qs, gs, de, dqa, s_scr, p_scr, dka, dva,
    s1, r1, s2, r2, s3, ps, pin, pown, pz, pall, pfin, len_s,
    loc, kv_send, kv_recv, qg_send, qg_recv, f_send, f_recv, o_send, o_recv,
    c_send, c_recv, x_send, x_recv, rs_send, rs_recv, cz_send, cz_recv, ag_send, ag_recv,
    fin, lead_sem, go_sem,
):
    c = lax.axis_index("ctx")
    r = lax.axis_index("resp")
    x, j = c // 4, c % 4
    zl, core = j // 2, j % 2
    core_mate = x * 4 + zl * 2 + (1 - core)
    z_mate = x * 4 + (1 - zl) * 2 + core
    j_c = zl * 2 + (1 - core)
    j_z = (1 - zl) * 2 + core
    ORDER = (1, 3, 2)
    ny = 4 if n == 16 else 2
    nz = n // ny
    ry, rz = r // nz, r % nz
    prow = 256 // ny
    nblk = 8 // ny

    def other(d):
        return (x + d) % 4

    def source(d):
        return (x + 4 - d) % 4

    def send(src, dst, ssem, rsem, **where):
        return pltpu.make_async_remote_copy(
            src_ref=src, dst_ref=dst, send_sem=ssem, recv_sem=rsem,
            device_id=where, device_id_type=MESH,
        )

    barrier = pltpu.get_barrier_semaphore()
    leader = c == 0
    near = [other(d) * 4 + j for d in ORDER] + [core_mate, z_mate]
    for to in near:

        @pl.when(to != 0)
        def _():
            pl.semaphore_signal(barrier, inc=1, device_id={"ctx": to}, device_id_type=MESH)

    by_leader = jnp.logical_or(j == 0, jnp.logical_and(x == 0, j < 3))

    @pl.when(jnp.logical_not(leader))
    def _():
        pl.semaphore_wait(barrier, 5)

        @pl.when(by_leader)
        def _():
            pl.semaphore_signal(lead_sem, inc=1, device_id={"ctx": 0}, device_id_type=MESH)

    @pl.when(leader)
    def _():
        pl.semaphore_wait(lead_sem, 5)

    def head_cols(h):
        return rows_of(h, DH)

    def kv_pairs(h, at):
        cols = head_cols(h)
        rows = rows_of(j, R)
        prows = pl.ds(pl.multiple_of(j * R + at * PR, PR), PR)
        return (
            (rk_ref.at[0, :, cols], kbuf.at[0, 1 + at, rows, :]),
            (rv_ref.at[0, :, cols], kbuf.at[1, 1 + at, rows, :]),
            (pk_ref.at[:, cols], kbuf.at[0, 0, prows, :]),
            (pv_ref.at[:, cols], kbuf.at[1, 0, prows, :]),
        )

    len_copy = pltpu.make_async_copy(len_ref, len_s, fin.at[6])
    len_copy.start()
    kv_copies = {}
    for d in ORDER:
        kv_copies[d] = [
            send(src, dst, kv_send.at[d - 1, i], kv_recv.at[d - 1, i], ctx=other(d) * 4 + j)
            for i, (src, dst) in enumerate(kv_pairs(other(d), x))
        ]
        for cp in kv_copies[d]:
            cp.start()
    own = [pltpu.make_async_copy(src, dst, loc.at[i]) for i, (src, dst) in enumerate(kv_pairs(x, x))]
    for cp in own:
        cp.start()

    def qg_pairs(h, at):
        cols = rows_of(h, GW)
        return ((q_ref.at[0, :, cols], qin.at[at]), (g_ref.at[0, :, cols], gin.at[at]))

    qg_copies = []
    for d in ORDER:
        for i, (src, dst) in enumerate(qg_pairs(other(d), x)):
            cp = send(src, dst, qg_send.at[d, i], qg_recv.at[d, i], ctx=other(d) * 4 + j)
            cp.start()
            qg_copies.append(cp)
    for i, (src, dst) in enumerate(qg_pairs(x, x)):
        pltpu.make_async_copy(src, dst, qg_recv.at[0, i]).start()

    fwd = []

    def hand_on(slot, chunk, rows_j, kind, mate):
        view = kbuf.at[:, chunk, rows_of(rows_j, R), :]
        cp = send(view, view, f_send.at[slot, kind], f_recv.at[slot, kind], ctx=mate)
        cp.start()
        fwd.append(cp)

    def wait_handed(slot, chunk, rows_j, kind, mate):
        view = kbuf.at[:, chunk, rows_of(rows_j, R), :]
        send(view, view, f_send.at[slot, kind], f_recv.at[slot, kind], ctx=mate).wait_recv()

    for cp in own:
        cp.wait()
    hand_on(0, 1 + x, j, 0, core_mate)
    hand_on(0, 1 + x, j, 1, z_mate)
    for d in ORDER:
        for i, (src, dst) in enumerate(kv_pairs(x, source(d))):
            send(src, dst, kv_send.at[d - 1, i], kv_recv.at[d - 1, i], ctx=c).wait_recv()
        hand_on(d, 1 + source(d), j, 0, core_mate)
        hand_on(d, 1 + source(d), j, 1, z_mate)
    hand_on(4, 0, j, 0, core_mate)
    hand_on(4, 0, j, 1, z_mate)
    slots = [(0, 1 + x)] + [(d, 1 + source(d)) for d in ORDER] + [(4, 0)]
    dka[...] = jnp.zeros_like(dka)
    dva[...] = jnp.zeros_like(dva)
    for slot, chunk in slots:
        wait_handed(slot, chunk, j_z, 1, z_mate)
        hand_on(slot, chunk, j_z, 2, core_mate)
    for slot, chunk in slots:
        wait_handed(slot, chunk, j_c, 0, core_mate)
        wait_handed(slot, chunk, 3 - j, 2, core_mate)

    @pl.when(leader)
    def _():
        for e in range(1, n):
            pl.semaphore_signal(barrier, inc=1, device_id={"resp": (r + e) % n}, device_id_type=MESH)

    def meet_responses():
        @pl.when(leader)
        def _():
            pl.semaphore_wait(barrier, n - 1)
            for to in range(1, 16):
                pl.semaphore_signal(go_sem, inc=1, device_id={"ctx": to}, device_id_type=MESH)

        @pl.when(jnp.logical_not(leader))
        def _():
            pl.semaphore_wait(go_sem, 1)

    len_copy.wait()
    length = len_s[0]

    def result_pairs(b, h):
        cols = rows_of(h, GW)
        return ((ob.at[b], out_ref.at[0, :, cols]), (dqb.at[b], dq_ref.at[0, :, cols]))

    def part(k, kv, jj):
        rows = rows_of(jj, R)
        if kv == 0:
            return dka[k, rows, :] * SCALE
        return dva[k, rows, :]

    def to_core(k):
        return send(s1.at[k], r1.at[k], c_send.at[0, k], c_recv.at[0, k], ctx=core_mate)

    def to_z(k):
        return send(s2.at[k], r2.at[k], c_send.at[1, k], c_recv.at[1, k], ctx=z_mate)

    def row_pairs(at, h):
        cols = head_cols(h)
        return ((s3.at[at, 0], drk_ref.at[0, :, cols]), (s3.at[at, 1], drv_ref.at[0, :, cols]))

    def scatter_copy(e):
        to = (ry + e) % ny
        return send(
            ps.at[rows_of(to, prow), :], pin.at[e], rs_send.at[e], rs_recv.at[e], resp=to * nz + rz
        )

    def cross_copy(e):
        to = (rz + e) % nz
        return send(pz.at[rz], pz.at[rz], cz_send.at[e], cz_recv.at[e], resp=ry * nz + to)

    def give_core(k):
        for kv in range(2):
            for zz in range(2):
                s1[k, zz, kv] = part(k, kv, 2 * zz + 1 - core).astype(BF)
        to_core(k).start()

    def give_z(k):
        to_core(k).wait_recv()
        for kv in range(2):
            s2[k, kv] = (part(k, kv, j_z) + r1[k, 1 - zl, kv].astype(F32)).astype(BF)
        to_z(k).start()

    def total(k, kv):
        return part(k, kv, j) + r1[k, zl, kv].astype(F32) + r2[k, kv].astype(F32)

    def give_prompt():
        to_z(0).wait_recv()
        for kv in range(2):
            t = total(0, kv)
            pown[kv * R : (kv + 1) * R, :] = t
            ps[kv * R : (kv + 1) * R, :] = t.astype(BF)
        meet_responses()
        for e in range(1, ny):
            scatter_copy(e).start()

    def give_x(k):
        to_z(k).wait_recv()
        at = k - 1
        for kv in range(2):
            s3[at, kv] = total(k, kv).astype(BF)

        @pl.when(at == x)
        def _():
            for t, (src, dst) in enumerate(row_pairs(at, x)):
                pltpu.make_async_copy(src, dst, fin.at[2 + t]).start()

        @pl.when(at != x)
        def _():
            d = (at + 4 - x) % 4
            for t, (src, dst) in enumerate(row_pairs(at, x)):
                send(src, dst, x_send.at[d, t], x_recv.at[d, t], ctx=at * 4 + j).start()

    def over(fn, low, high):
        lax.fori_loop(low, high, lambda k, carry: (fn(k), carry)[1], 0)

    def cross_prompt():
        acc = pown[rows_of(ry, prow), :]
        for e in range(1, ny):
            scatter_copy(e).wait_recv()
            acc = acc + pin[e].astype(F32)
        pz[rz] = acc.astype(BF)
        for e in range(1, nz):
            cross_copy(e).start()

    def piece_copy(e, t):
        g = ry * nblk + t
        kv, at = g // 4, g % 4
        src = pall.at[pl.ds(t * PR, PR), :]
        dst = pfin.at[kv, :, head_cols(x)]
        rsem = ag_recv.at[kv, x]
        away = send(
            src, dst, ag_send.at[e, t], rsem, resp=((ry + e) % ny) * nz + rz, ctx=at * 4 + j
        )
        return away, pltpu.make_async_copy(src, dst, rsem), at

    def sum_prompt():
        for e in range(1, nz):
            came = pz.at[(rz + nz - e) % nz]
            send(came, came, cz_send.at[e], cz_recv.at[e], resp=r).wait_recv()
        acc = pz[0].astype(F32)
        for z in range(1, nz):
            acc = acc + pz[z].astype(F32)
        pall[...] = acc.astype(BF)
        for e in range(ny):
            for t in range(nblk):
                away, home, at = piece_copy(e, t)
                if e:
                    away.start()
                else:
                    pl.when(at == x)(home.start)
                    pl.when(at != x)(away.start)

    def step(i, carry):
        d = jnp.where(i == 0, 0, jnp.where(i == 1, 1, jnp.where(i == 2, 3, 2)))
        b = (x + 4 - d) % 4
        for t, (src, dst) in enumerate(qg_pairs(x, b)):
            pltpu.make_async_copy(src, dst, qg_recv.at[d, t]).wait()
        for bb in range(4):

            @pl.when(b == bb)
            def _():
                attend_block(bb, j, length, qin, gin, kbuf, ob, qs, gs, de, s_scr, p_scr)

        src, dst = result_pairs(b, x)[0]

        @pl.when(i == 0)
        def _():
            pltpu.make_async_copy(src, dst, fin.at[0]).start()

        @pl.when(i > 0)
        def _():
            send(src, dst, o_send.at[d, 0], o_recv.at[d, 0], ctx=b * 4 + j).start()

        return carry

    lax.fori_loop(0, 4, step, 0)

    def terms(k, rows):
        return grad_terms(k, rows, kbuf, qs, gs, de, p_scr, dka, dva)

    for b in range(4):
        rows = slice(b * M, (b + 1) * M)
        dqa[rows, :] = terms(0, rows)
    give_core(0)

    ends = []
    for d in (2, 1, 3):
        ends.append((ends[-1] if ends else 0) + source(d) + 1)

    def unit(u, carry):
        past = [u >= end for end in ends]
        d = jnp.where(past[2], 0, jnp.where(past[1], 3, jnp.where(past[0], 1, 2)))
        begin = jnp.where(past[2], ends[2], jnp.where(past[1], ends[1], jnp.where(past[0], ends[0], 0)))
        b = (x + 4 - d) % 4
        k = u - begin + 1
        rows = rows_of(b, M)
        dqa[rows, :] += terms(k, rows)
        own = d == 0

        @pl.when(own)
        def _():
            give_core(k)

        @pl.when(k == b + 1)
        def _():
            for h in range(G):
                dq = dqa[pl.ds(pl.multiple_of(b * M + h * R, R), R), :]
                dqb[b, :, h * DH : (h + 1) * DH] = (dq * SCALE).astype(BF)
            src, dst = result_pairs(b, x)[1]

            @pl.when(own)
            def _():
                pltpu.make_async_copy(src, dst, fin.at[1]).start()

            @pl.when(jnp.logical_not(own))
            def _():
                send(src, dst, o_send.at[d, 1], o_recv.at[d, 1], ctx=b * 4 + j).start()

        @pl.when(u == 0)
        def _():
            give_z(0)

        @pl.when(u == 3)
        def _():
            give_prompt()

        @pl.when(u + 1 == ends[2])
        def _():
            over(give_core, x + 2, NC)

        @pl.when(jnp.logical_and(own, k == 1))
        def _():
            over(give_z, x + 2, NC)

        @pl.when(jnp.logical_and(own, k >= 2))
        def _():
            give_z(k - 1)

        @pl.when(jnp.logical_and(own, k == 3))
        def _():
            over(give_x, x + 2, NC)

        @pl.when(jnp.logical_and(own, k >= 3))
        def _():
            give_x(k - 2)

        @pl.when(u == 6)
        def _():
            cross_prompt()

        return carry

    lax.fori_loop(0, 10, unit, 0)
    give_z(x + 1)

    @pl.when(x < 2)
    def _():
        over(give_x, x + 2, NC)

    sum_prompt()
    over(give_x, jnp.maximum(x, 1), x + 2)
    finals = [pltpu.make_async_copy(src, dst, fin.at[t]) for t, (src, dst) in enumerate(result_pairs(x, x))]
    for kv in range(2):
        for h in range(4):
            src, dst = pall.at[pl.ds(0, PR), :], pfin.at[kv, :, head_cols(h)]
            pltpu.make_async_copy(src, dst, ag_recv.at[kv, h]).wait()
    for kv, dst in enumerate((dpk_ref, dpv_ref)):
        cp = pltpu.make_async_copy(pfin.at[kv], dst, fin.at[4 + kv])
        cp.start()
        finals.append(cp)
    for t, (src, dst) in enumerate(row_pairs(x, x)):
        finals.append(pltpu.make_async_copy(src, dst, fin.at[2 + t]))

    for d in ORDER:
        for t in range(2):
            src, dst = result_pairs(source(d), other(d))[t]
            cp = send(src, dst, o_send.at[d, t], o_recv.at[d, t], ctx=source(d) * 4 + j)
            cp.wait_recv()
            cp.wait_send()
            src, dst = row_pairs(x, source(d))[t]
            cp = send(src, dst, x_send.at[d, t], x_recv.at[d, t], ctx=c)
            cp.wait_recv()
            cp.wait_send()
    for cp in finals:
        cp.wait()
    for d in ORDER:
        for cp in kv_copies[d]:
            cp.wait_send()
    for cp in qg_copies + fwd:
        cp.wait_send()
    for k in range(NC):
        to_core(k).wait_send()
        to_z(k).wait_send()

    for e in range(1, ny):
        scatter_copy(e).wait_send()
    for e in range(1, nz):
        cross_copy(e).wait_send()
    for e in range(ny):
        for t in range(nblk):
            away, home, at = piece_copy(e, t)
            if e:
                away.wait_send()
            else:
                pl.when(at != x)(away.wait_send)


def finish(*refs):
    ins, outs, sems = refs[:6], refs[6:12], refs[12]
    copies = [pltpu.make_async_copy(src, dst, sems.at[i]) for i, (src, dst) in enumerate(zip(ins, outs))]
    for cp in copies:
        cp.start()
    for cp in copies:
        cp.wait()


def body(n, queries, resp_keys, resp_values, prompt_keys, prompt_values, out_grad, lengths):
    shape = jax.ShapeDtypeStruct
    ny = 4 if n == 16 else 2
    anywhere = pl.BlockSpec(memory_space=pl.ANY)
    vmem = pltpu.VMEM
    dma = pltpu.SemaphoreType.DMA
    outs = (
        shape((1, R, HQ * DH), BF),
        shape((1, R, HQ * DH), BF),
        shape((1, R, HK * DH), BF),
        shape((1, R, HK * DH), BF),
        shape((PR, HK * DH), BF),
        shape((PR, HK * DH), BF),
    )
    results = pl.pallas_call(
        functools.partial(kernel, n),
        out_shape=outs,
        in_specs=[anywhere] * 7,
        out_specs=(anywhere,) * 6,
        scratch_shapes=[
            vmem((4, R, GW), BF), vmem((4, R, GW), BF), vmem((2, NC, CH, DH), BF),
            vmem((4, R, GW), BF), vmem((4, R, GW), BF), vmem((4 * M, DH), BF), vmem((4 * M, DH), BF),
            vmem((4 * M, 128), F32), vmem((4 * M, DH), F32),
            vmem((NC, M, CH), F32), vmem((NC, 4 * M, CH), BF), vmem((NC, CH, DH), F32), vmem((NC, CH, DH), F32),
            vmem((NC, 2, 2, R, DH), BF), vmem((NC, 2, 2, R, DH), BF),
            vmem((NC, 2, R, DH), BF), vmem((NC, 2, R, DH), BF), vmem((4, 2, R, DH), BF),
            vmem((2 * R, DH), BF), vmem((ny, 256 // ny, DH), BF), vmem((2 * R, DH), F32),
            vmem((n // ny, 256 // ny, DH), BF), vmem((256 // ny, DH), BF),
            vmem((2, PR, HK * DH), BF),
            pltpu.SMEM((1,), jnp.int32),
            dma((4,)), dma((3, 4)), dma((3, 4)), dma((4, 2)), dma((4, 2)), dma((5, 3)), dma((5, 3)),
            dma((4, 2)), dma((4, 2)), dma((2, NC)), dma((2, NC)), dma((4, 2)), dma((4, 2)),
            dma((ny,)), dma((ny,)), dma((n // ny,)), dma((n // ny,)), dma((ny, 8 // ny)), dma((2, 4)), dma((7,)),
            pltpu.SemaphoreType.REGULAR, pltpu.SemaphoreType.REGULAR,
        ],
        compiler_params=pltpu.CompilerParams(
            collective_id=0, has_side_effects=True, vmem_limit_bytes=56 << 20
        ),
    )(lengths, queries, resp_keys, resp_values, prompt_keys, prompt_values, out_grad)
    return pl.pallas_call(
        finish,
        out_shape=outs,
        in_specs=[pl.BlockSpec(memory_space=vmem)] * 6,
        out_specs=(anywhere,) * 6,
        scratch_shapes=[dma((6,))],
    )(*results)


def solution(mesh):
    seq = P("resp", "ctx", None)
    return jax.shard_map(
        functools.partial(body, mesh.shape["resp"]),
        mesh=mesh,
        in_specs=(seq, seq, seq, P("ctx", None), P("ctx", None), seq, P("resp")),
        out_specs=(seq, seq, seq, seq, P("ctx", None), P("ctx", None)),
        check_vma=False,
    )
```

```python
import functools
import math

import jax
import jax.numpy as jnp
from jax import lax
from jax.experimental import pallas as pl
from jax.experimental.pallas import tpu as pltpu
from jax.sharding import PartitionSpec as P

DH = 128
HQ = 20
HK = 4
G = HQ // HK
GW = G * DH
R = 128
M = G * R
CH = 512
NC = 5
PR = 32
BF = jnp.bfloat16
F32 = jnp.float32
MESH = pl.DeviceIdType.MESH
SCALE = DH**-0.5
CEXP = SCALE * math.log2(math.e)
NEG = -1e30
NT = (((1,), (1,)), ((), ()))
NN = (((1,), (0,)), ((), ()))
TN = (((0,), (0,)), ((), ()))


def dot(a, b, dims):
    return lax.dot_general(a, b, dims, preferred_element_type=F32)


def rows_of(i, size):
    return pl.ds(pl.multiple_of(i * size, size), size)


def attend_block(b, j, length, qin, gin, kbuf, ob, qs, gs, de, s_scr, p_scr):
    base = b * M
    mine = slice(base, base + M)
    last = b + 1
    for h in range(G):
        qs[base + h * R : base + (h + 1) * R, :] = qin[b, :, h * DH : (h + 1) * DH]
    q = qs[mine, :]
    row = lax.broadcasted_iota(jnp.int32, (R, 128), 0) + j * R
    col = lax.broadcasted_iota(jnp.int32, (R, 128), 1)
    m = jnp.full((M, 128), NEG, F32)
    for k in range(last + 1):
        s = dot(q, kbuf[0, k], NT)
        for t in range(0, CH, 128):
            part = s[:, t : t + 128]
            if k == last:
                part = jnp.where(jnp.concatenate([col + t <= row] * G, axis=0), part, NEG)
            s_scr[k, :, t : t + 128] = part
            m = jnp.maximum(m, part)
    top = jnp.broadcast_to(jnp.max(m, axis=1, keepdims=True) * CEXP, (M, 128))
    o = jnp.zeros((M, DH), F32)
    l = jnp.zeros((M, 128), F32)
    for k in range(last + 1):
        ps = []
        for t in range(0, CH, 128):
            p = jnp.exp2(s_scr[k, :, t : t + 128] * CEXP - top)
            l = l + p
            ps.append(p.astype(BF))
        p = jnp.concatenate(ps, axis=1)
        p_scr[k, mine, :] = p
        o = o + dot(p, kbuf[1, k], NN)
    rl = 1.0 / jnp.sum(l, axis=1, keepdims=True)
    token = lax.broadcasted_iota(jnp.int32, (R, 1), 0) + (4 * b + j) * R
    valid = jnp.concatenate([token < length] * G, axis=0)
    o = jnp.where(valid, o * rl, 0.0).astype(BF)
    for h in range(G):
        ob[b, :, h * DH : (h + 1) * DH] = o[h * R : (h + 1) * R, :]
        gs[base + h * R : base + (h + 1) * R, :] = gin[b, :, h * DH : (h + 1) * DH]
    gl = jnp.where(valid, gs[mine, :].astype(F32) * rl, 0.0).astype(BF)
    gs[mine, :] = gl
    delta = jnp.sum(gl.astype(F32) * o.astype(F32), axis=1, keepdims=True)
    de[mine, :] = jnp.broadcast_to(delta, (M, 128))


def grad_terms(k, rows, kbuf, qs, gs, de, p_scr, dka, dva):
    gl = gs[rows, :]
    delta = de[rows, :]
    p = p_scr[k, rows, :]
    dp = dot(gl, kbuf[1, k], NT)
    ds = jnp.concatenate(
        [
            (p[:, t : t + 128].astype(F32) * (dp[:, t : t + 128] - delta)).astype(BF)
            for t in range(0, CH, 128)
        ],
        axis=1,
    )
    dva[k] += dot(p, gl, TN)
    dka[k] += dot(ds, qs[rows, :], TN)
    return dot(ds, kbuf[0, k], NN)


def kernel(
    n,
    len_ref, q_ref, rk_ref, rv_ref, pk_ref, pv_ref, g_ref,
    out_ref, dq_ref, drk_ref, drv_ref, dpk_ref, dpv_ref,
    qin, gin, kbuf, ob, dqb, qs, gs, de, dqa, s_scr, p_scr, dka, dva,
    s1, r1, s2, r2, s3, ps, pin, pown, pz, pall, pfin, len_s,
    loc, kv_send, kv_recv, qg_send, qg_recv, f_send, f_recv, o_send, o_recv,
    c_send, c_recv, x_send, x_recv, rs_send, rs_recv, cz_send, cz_recv, ag_send, ag_recv,
    fin, lead_sem, go_sem,
):
    c = lax.axis_index("ctx")
    r = lax.axis_index("resp")
    x, j = c // 4, c % 4
    zl, core = j // 2, j % 2
    core_mate = x * 4 + zl * 2 + (1 - core)
    z_mate = x * 4 + (1 - zl) * 2 + core
    j_c = zl * 2 + (1 - core)
    j_z = (1 - zl) * 2 + core
    ORDER = (1, 3, 2)
    ny = 4 if n == 16 else 2
    nz = n // ny
    ry, rz = r // nz, r % nz
    prow = 256 // ny
    nblk = 8 // ny

    def other(d):
        return (x + d) % 4

    def source(d):
        return (x + 4 - d) % 4

    def send(src, dst, ssem, rsem, **where):
        return pltpu.make_async_remote_copy(
            src_ref=src, dst_ref=dst, send_sem=ssem, recv_sem=rsem,
            device_id=where, device_id_type=MESH,
        )

    barrier = pltpu.get_barrier_semaphore()
    leader = c == 0
    near = [other(d) * 4 + j for d in ORDER] + [core_mate, z_mate]
    for to in near:

        @pl.when(to != 0)
        def _():
            pl.semaphore_signal(barrier, inc=1, device_id={"ctx": to}, device_id_type=MESH)

    by_leader = jnp.logical_or(j == 0, jnp.logical_and(x == 0, j < 3))

    @pl.when(jnp.logical_not(leader))
    def _():
        pl.semaphore_wait(barrier, 5)

        @pl.when(by_leader)
        def _():
            pl.semaphore_signal(lead_sem, inc=1, device_id={"ctx": 0}, device_id_type=MESH)

    @pl.when(leader)
    def _():
        pl.semaphore_wait(lead_sem, 5)

    def head_cols(h):
        return rows_of(h, DH)

    def kv_pairs(h, at):
        cols = head_cols(h)
        rows = rows_of(j, R)
        prows = pl.ds(pl.multiple_of(j * R + at * PR, PR), PR)
        return (
            (rk_ref.at[0, :, cols], kbuf.at[0, 1 + at, rows, :]),
            (rv_ref.at[0, :, cols], kbuf.at[1, 1 + at, rows, :]),
            (pk_ref.at[:, cols], kbuf.at[0, 0, prows, :]),
            (pv_ref.at[:, cols], kbuf.at[1, 0, prows, :]),
        )

    len_copy = pltpu.make_async_copy(len_ref, len_s, fin.at[6])
    len_copy.start()
    kv_copies = {}
    for d in ORDER:
        kv_copies[d] = [
            send(src, dst, kv_send.at[d - 1, i], kv_recv.at[d - 1, i], ctx=other(d) * 4 + j)
            for i, (src, dst) in enumerate(kv_pairs(other(d), x))
        ]
        for cp in kv_copies[d]:
            cp.start()
    own = [pltpu.make_async_copy(src, dst, loc.at[i]) for i, (src, dst) in enumerate(kv_pairs(x, x))]
    for cp in own:
        cp.start()

    def qg_pairs(h, at):
        cols = rows_of(h, GW)
        return ((q_ref.at[0, :, cols], qin.at[at]), (g_ref.at[0, :, cols], gin.at[at]))

    qg_copies = []
    for d in ORDER:
        for i, (src, dst) in enumerate(qg_pairs(other(d), x)):
            cp = send(src, dst, qg_send.at[d, i], qg_recv.at[d, i], ctx=other(d) * 4 + j)
            cp.start()
            qg_copies.append(cp)
    for i, (src, dst) in enumerate(qg_pairs(x, x)):
        pltpu.make_async_copy(src, dst, qg_recv.at[0, i]).start()

    fwd = []

    def hand_on(slot, chunk, rows_j, kind, mate):
        view = kbuf.at[:, chunk, rows_of(rows_j, R), :]
        cp = send(view, view, f_send.at[slot, kind], f_recv.at[slot, kind], ctx=mate)
        cp.start()
        fwd.append(cp)

    def wait_handed(slot, chunk, rows_j, kind, mate):
        view = kbuf.at[:, chunk, rows_of(rows_j, R), :]
        send(view, view, f_send.at[slot, kind], f_recv.at[slot, kind], ctx=mate).wait_recv()

    for cp in own:
        cp.wait()
    hand_on(0, 1 + x, j, 0, core_mate)
    hand_on(0, 1 + x, j, 1, z_mate)
    for d in ORDER:
        for i, (src, dst) in enumerate(kv_pairs(x, source(d))):
            send(src, dst, kv_send.at[d - 1, i], kv_recv.at[d - 1, i], ctx=c).wait_recv()
        hand_on(d, 1 + source(d), j, 0, core_mate)
        hand_on(d, 1 + source(d), j, 1, z_mate)
    hand_on(4, 0, j, 0, core_mate)
    hand_on(4, 0, j, 1, z_mate)
    slots = [(0, 1 + x)] + [(d, 1 + source(d)) for d in ORDER] + [(4, 0)]
    dka[...] = jnp.zeros_like(dka)
    dva[...] = jnp.zeros_like(dva)
    for slot, chunk in slots:
        wait_handed(slot, chunk, j_z, 1, z_mate)
        hand_on(slot, chunk, j_z, 2, core_mate)
    for slot, chunk in slots:
        wait_handed(slot, chunk, j_c, 0, core_mate)
        wait_handed(slot, chunk, 3 - j, 2, core_mate)

    @pl.when(leader)
    def _():
        for e in range(1, n):
            pl.semaphore_signal(barrier, inc=1, device_id={"resp": (r + e) % n}, device_id_type=MESH)

    def meet_responses():
        @pl.when(leader)
        def _():
            pl.semaphore_wait(barrier, n - 1)
            for to in range(1, 16):
                pl.semaphore_signal(go_sem, inc=1, device_id={"ctx": to}, device_id_type=MESH)

        @pl.when(jnp.logical_not(leader))
        def _():
            pl.semaphore_wait(go_sem, 1)

    len_copy.wait()
    length = len_s[0]

    def result_pairs(b, h):
        cols = rows_of(h, GW)
        return ((ob.at[b], out_ref.at[0, :, cols]), (dqb.at[b], dq_ref.at[0, :, cols]))

    def part(k, kv, jj):
        rows = rows_of(jj, R)
        if kv == 0:
            return dka[k, rows, :] * SCALE
        return dva[k, rows, :]

    def to_core(k):
        return send(s1.at[k], r1.at[k], c_send.at[0, k], c_recv.at[0, k], ctx=core_mate)

    def to_z(k):
        return send(s2.at[k], r2.at[k], c_send.at[1, k], c_recv.at[1, k], ctx=z_mate)

    def row_pairs(at, h):
        cols = head_cols(h)
        return ((s3.at[at, 0], drk_ref.at[0, :, cols]), (s3.at[at, 1], drv_ref.at[0, :, cols]))

    def scatter_copy(e):
        to = (ry + e) % ny
        return send(
            ps.at[rows_of(to, prow), :], pin.at[e], rs_send.at[e], rs_recv.at[e], resp=to * nz + rz
        )

    def cross_copy(e):
        to = (rz + e) % nz
        return send(pz.at[rz], pz.at[rz], cz_send.at[e], cz_recv.at[e], resp=ry * nz + to)

    def give_core(k):
        for kv in range(2):
            for zz in range(2):
                s1[k, zz, kv] = part(k, kv, 2 * zz + 1 - core).astype(BF)
        to_core(k).start()

    def give_z(k):
        to_core(k).wait_recv()
        for kv in range(2):
            s2[k, kv] = (part(k, kv, j_z) + r1[k, 1 - zl, kv].astype(F32)).astype(BF)
        to_z(k).start()

    def total(k, kv):
        return part(k, kv, j) + r1[k, zl, kv].astype(F32) + r2[k, kv].astype(F32)

    def give_prompt():
        to_z(0).wait_recv()
        for kv in range(2):
            t = total(0, kv)
            pown[kv * R : (kv + 1) * R, :] = t
            ps[kv * R : (kv + 1) * R, :] = t.astype(BF)
        meet_responses()
        for e in range(1, ny):
            scatter_copy(e).start()

    def give_x(k):
        to_z(k).wait_recv()
        at = k - 1
        for kv in range(2):
            s3[at, kv] = total(k, kv).astype(BF)

        @pl.when(at == x)
        def _():
            for t, (src, dst) in enumerate(row_pairs(at, x)):
                pltpu.make_async_copy(src, dst, fin.at[2 + t]).start()

        @pl.when(at != x)
        def _():
            d = (at + 4 - x) % 4
            for t, (src, dst) in enumerate(row_pairs(at, x)):
                send(src, dst, x_send.at[d, t], x_recv.at[d, t], ctx=at * 4 + j).start()

    def over(fn, low, high):
        lax.fori_loop(low, high, lambda k, carry: (fn(k), carry)[1], 0)

    def cross_prompt():
        acc = pown[rows_of(ry, prow), :]
        for e in range(1, ny):
            scatter_copy(e).wait_recv()
            acc = acc + pin[e].astype(F32)
        pz[rz] = acc.astype(BF)
        for e in range(1, nz):
            cross_copy(e).start()

    def piece_copy(e, t):
        g = ry * nblk + t
        kv, at = g // 4, g % 4
        src = pall.at[pl.ds(t * PR, PR), :]
        dst = pfin.at[kv, :, head_cols(x)]
        rsem = ag_recv.at[kv, x]
        away = send(
            src, dst, ag_send.at[e, t], rsem, resp=((ry + e) % ny) * nz + rz, ctx=at * 4 + j
        )
        return away, pltpu.make_async_copy(src, dst, rsem), at

    def sum_prompt():
        for e in range(1, nz):
            came = pz.at[(rz + nz - e) % nz]
            send(came, came, cz_send.at[e], cz_recv.at[e], resp=r).wait_recv()
        acc = pz[0].astype(F32)
        for z in range(1, nz):
            acc = acc + pz[z].astype(F32)
        pall[...] = acc.astype(BF)
        for e in range(ny):
            for t in range(nblk):
                away, home, at = piece_copy(e, t)
                if e:
                    away.start()
                else:
                    pl.when(at == x)(home.start)
                    pl.when(at != x)(away.start)

    def step(i, carry):
        d = jnp.where(i == 0, 0, jnp.where(i == 1, 1, jnp.where(i == 2, 3, 2)))
        b = (x + 4 - d) % 4
        for t, (src, dst) in enumerate(qg_pairs(x, b)):
            pltpu.make_async_copy(src, dst, qg_recv.at[d, t]).wait()
        for bb in range(4):

            @pl.when(b == bb)
            def _():
                attend_block(bb, j, length, qin, gin, kbuf, ob, qs, gs, de, s_scr, p_scr)

        src, dst = result_pairs(b, x)[0]

        @pl.when(i == 0)
        def _():
            pltpu.make_async_copy(src, dst, fin.at[0]).start()

        @pl.when(i > 0)
        def _():
            send(src, dst, o_send.at[d, 0], o_recv.at[d, 0], ctx=b * 4 + j).start()

        return carry

    lax.fori_loop(0, 4, step, 0)

    def terms(k, rows):
        return grad_terms(k, rows, kbuf, qs, gs, de, p_scr, dka, dva)

    for b in range(4):
        rows = slice(b * M, (b + 1) * M)
        dqa[rows, :] = terms(0, rows)
    give_core(0)

    ends = []
    for d in (2, 1, 3):
        ends.append((ends[-1] if ends else 0) + source(d) + 1)

    def unit(u, carry):
        past = [u >= end for end in ends]
        d = jnp.where(past[2], 0, jnp.where(past[1], 3, jnp.where(past[0], 1, 2)))
        begin = jnp.where(past[2], ends[2], jnp.where(past[1], ends[1], jnp.where(past[0], ends[0], 0)))
        b = (x + 4 - d) % 4
        k = u - begin + 1
        rows = rows_of(b, M)
        dqa[rows, :] += terms(k, rows)
        own = d == 0

        @pl.when(own)
        def _():
            give_core(k)

        @pl.when(k == b + 1)
        def _():
            for h in range(G):
                dq = dqa[pl.ds(pl.multiple_of(b * M + h * R, R), R), :]
                dqb[b, :, h * DH : (h + 1) * DH] = (dq * SCALE).astype(BF)
            src, dst = result_pairs(b, x)[1]

            @pl.when(own)
            def _():
                pltpu.make_async_copy(src, dst, fin.at[1]).start()

            @pl.when(jnp.logical_not(own))
            def _():
                send(src, dst, o_send.at[d, 1], o_recv.at[d, 1], ctx=b * 4 + j).start()

        @pl.when(u == 0)
        def _():
            give_z(0)

        @pl.when(u == 3)
        def _():
            give_prompt()

        @pl.when(u + 1 == ends[2])
        def _():
            over(give_core, x + 2, NC)

        @pl.when(jnp.logical_and(own, k == 1))
        def _():
            over(give_z, x + 2, NC)

        @pl.when(jnp.logical_and(own, k >= 2))
        def _():
            give_z(k - 1)

        @pl.when(jnp.logical_and(own, k == 3))
        def _():
            over(give_x, x + 2, NC)

        @pl.when(jnp.logical_and(own, k >= 3))
        def _():
            give_x(k - 2)

        @pl.when(u == 6)
        def _():
            cross_prompt()

        return carry

    lax.fori_loop(0, 10, unit, 0)
    give_z(x + 1)

    sum_prompt()

    @pl.when(x < 2)
    def _():
        over(give_x, x + 2, NC)

    over(give_x, jnp.maximum(x, 1), x + 2)
    finals = [pltpu.make_async_copy(src, dst, fin.at[t]) for t, (src, dst) in enumerate(result_pairs(x, x))]
    for kv in range(2):
        for h in range(4):
            src, dst = pall.at[pl.ds(0, PR), :], pfin.at[kv, :, head_cols(h)]
            pltpu.make_async_copy(src, dst, ag_recv.at[kv, h]).wait()
    for kv, dst in enumerate((dpk_ref, dpv_ref)):
        cp = pltpu.make_async_copy(pfin.at[kv], dst, fin.at[4 + kv])
        cp.start()
        finals.append(cp)
    for t, (src, dst) in enumerate(row_pairs(x, x)):
        finals.append(pltpu.make_async_copy(src, dst, fin.at[2 + t]))

    for d in ORDER:
        for t in range(2):
            src, dst = result_pairs(source(d), other(d))[t]
            cp = send(src, dst, o_send.at[d, t], o_recv.at[d, t], ctx=source(d) * 4 + j)
            cp.wait_recv()
            cp.wait_send()
            src, dst = row_pairs(x, source(d))[t]
            cp = send(src, dst, x_send.at[d, t], x_recv.at[d, t], ctx=c)
            cp.wait_recv()
            cp.wait_send()
    for cp in finals:
        cp.wait()
    for d in ORDER:
        for cp in kv_copies[d]:
            cp.wait_send()
    for cp in qg_copies + fwd:
        cp.wait_send()
    for k in range(NC):
        to_core(k).wait_send()
        to_z(k).wait_send()

    for e in range(1, ny):
        scatter_copy(e).wait_send()
    for e in range(1, nz):
        cross_copy(e).wait_send()
    for e in range(ny):
        for t in range(nblk):
            away, home, at = piece_copy(e, t)
            if e:
                away.wait_send()
            else:
                pl.when(at != x)(away.wait_send)


def finish(*refs):
    ins, outs, sems = refs[:6], refs[6:12], refs[12]
    copies = [pltpu.make_async_copy(src, dst, sems.at[i]) for i, (src, dst) in enumerate(zip(ins, outs))]
    for cp in copies:
        cp.start()
    for cp in copies:
        cp.wait()


def body(n, queries, resp_keys, resp_values, prompt_keys, prompt_values, out_grad, lengths):
    shape = jax.ShapeDtypeStruct
    ny = 4 if n == 16 else 2
    anywhere = pl.BlockSpec(memory_space=pl.ANY)
    vmem = pltpu.VMEM
    dma = pltpu.SemaphoreType.DMA
    outs = (
        shape((1, R, HQ * DH), BF),
        shape((1, R, HQ * DH), BF),
        shape((1, R, HK * DH), BF),
        shape((1, R, HK * DH), BF),
        shape((PR, HK * DH), BF),
        shape((PR, HK * DH), BF),
    )
    results = pl.pallas_call(
        functools.partial(kernel, n),
        out_shape=outs,
        in_specs=[anywhere] * 7,
        out_specs=(anywhere,) * 6,
        scratch_shapes=[
            vmem((4, R, GW), BF), vmem((4, R, GW), BF), vmem((2, NC, CH, DH), BF),
            vmem((4, R, GW), BF), vmem((4, R, GW), BF), vmem((4 * M, DH), BF), vmem((4 * M, DH), BF),
            vmem((4 * M, 128), F32), vmem((4 * M, DH), F32),
            vmem((NC, M, CH), F32), vmem((NC, 4 * M, CH), BF), vmem((NC, CH, DH), F32), vmem((NC, CH, DH), F32),
            vmem((NC, 2, 2, R, DH), BF), vmem((NC, 2, 2, R, DH), BF),
            vmem((NC, 2, R, DH), BF), vmem((NC, 2, R, DH), BF), vmem((4, 2, R, DH), BF),
            vmem((2 * R, DH), BF), vmem((ny, 256 // ny, DH), BF), vmem((2 * R, DH), F32),
            vmem((n // ny, 256 // ny, DH), BF), vmem((256 // ny, DH), BF),
            vmem((2, PR, HK * DH), BF),
            pltpu.SMEM((1,), jnp.int32),
            dma((4,)), dma((3, 4)), dma((3, 4)), dma((4, 2)), dma((4, 2)), dma((5, 3)), dma((5, 3)),
            dma((4, 2)), dma((4, 2)), dma((2, NC)), dma((2, NC)), dma((4, 2)), dma((4, 2)),
            dma((ny,)), dma((ny,)), dma((n // ny,)), dma((n // ny,)), dma((ny, 8 // ny)), dma((2, 4)), dma((7,)),
            pltpu.SemaphoreType.REGULAR, pltpu.SemaphoreType.REGULAR,
        ],
        compiler_params=pltpu.CompilerParams(
            collective_id=0, has_side_effects=True, vmem_limit_bytes=56 << 20
        ),
    )(lengths, queries, resp_keys, resp_values, prompt_keys, prompt_values, out_grad)
    return pl.pallas_call(
        finish,
        out_shape=outs,
        in_specs=[pl.BlockSpec(memory_space=vmem)] * 6,
        out_specs=(anywhere,) * 6,
        scratch_shapes=[dma((6,))],
    )(*results)


def solution(mesh):
    seq = P("resp", "ctx", None)
    return jax.shard_map(
        functools.partial(body, mesh.shape["resp"]),
        mesh=mesh,
        in_specs=(seq, seq, seq, P("ctx", None), P("ctx", None), seq, P("resp")),
        out_specs=(seq, seq, seq, seq, P("ctx", None), P("ctx", None)),
        check_vma=False,
    )
```
